32 devices in a mesh: dp: 4 (over y, core), expert: 8 (over z, x).
Axes of the slice: x: 2, y: 2, z: 4, core: 2. Of those that a mesh axis runs over, the one named last changes fastest.
Arguments:
- tokens: bfloat16 [4096, 3584], P(('dp', 'expert')), may hold values from -6 to 6
- cotangent: bfloat16 [4096, 3584], P(('dp', 'expert')), may hold values from -1.5 to 1.5
- gates: bfloat16 [4096, 2], P(('dp', 'expert')), may hold values from 0.19921875 to 1
- expert_ids: int32 [4096, 2], P(('dp', 'expert')), may hold values from 0 to 7, all different within a row; in each aligned block of 128 rows (0 to 127, 128 to 255, ...) at most 48 rows name the same one
- gate_w: bfloat16 [8, 3584, 1024], P('expert'), may hold values from -0.09375 to 0.09375
- up_w: bfloat16 [8, 3584, 1024], P('expert'), may hold values from -0.09375 to 0.09375
- down_w: bfloat16 [8, 1024, 3584], P('expert'), may hold values from -0.1875 to 0.1875
Outputs:
- grad_tokens: bfloat16 [4096, 3584], P('dp', 'expert')
- grad_gate_w: bfloat16 [8, 3584, 1024], P('expert', 'dp')
- grad_up_w: bfloat16 [8, 3584, 1024], P('expert', 'dp')
- grad_gates: bfloat16 [4096, 2], P(('dp', 'expert'))
The draws below stay inside these ranges and needn't reach their ends.
Inputs may be any that keep to these rules, and one draw needn't show every extreme that they name: `expert_ids`: each token names 2 different experts; among the 128 tokens of one device no expert is named more than 48 times, and in every draw some expert is named exactly 48 times by some device's tokens.
All inputs are finite; a program needn't handle non-finite values.
Results may differ from the reference program's by a relative error of at most 0.014.
Values may be sent and summed in bfloat16 or wider, within the bound.
No kernel may reach another device: no remote copies, remote signals or barrier semaphores. Data moves between devices by JAX's collectives and lax.ppermute only.
A program may use at most 192 MiB of HBM per device.

```python
import math
import jax
import jax.numpy as jnp
import numpy as np
from jax import lax

D = 3584
H = 1024
TOP = 2
TOK_DEV = 128
EXPERTS = 8
CAP = 48
TOKENS = 4096
N_DP = 4
N_EXPERT = 8


def strengthened(array, own_key, source, target, parts, factor):
    def block_of(axis_at):
        return (jnp.arange(array.shape[axis_at]) // (array.shape[axis_at] // parts)).reshape((-1,) + (1,) * (array.ndim - 1 - axis_at))

    first = jax.random.permutation(own_key, parts)[block_of(target)]
    other_side = (block_of(target) + parts // 2) % parts
    return jnp.where((block_of(source) == first) | (block_of(source) == other_side), factor * array, array)


def level_of(own_key, dims, split, low, high):
    def one(axis_at, parts):
        heights = jax.random.uniform(jax.random.fold_in(jax.random.fold_in(own_key, 6), axis_at), (parts,), jnp.float32, low / len(split), high / len(split))
        return jnp.repeat(jnp.exp(heights), dims[axis_at] // parts).reshape((-1,) + (1,) * (len(dims) - axis_at - 1))

    factor_of = one(*split[0])
    for cut in split[1:]:
        factor_of = factor_of * one(*cut)
    return factor_of


def deal_out(rng, own, number, rows, amount, top, limit, lean):
    order = jax.random.permutation(rng, amount)
    heavy_load, common = portions_of(amount, rows * top, limit, lean, True), portions_of(amount, rows * top, limit, lean, False)
    places = jnp.arange(amount)

    def named(sizes, rotation):
        used = int((sizes > 0).sum())
        fixed = max(1, used // 4)
        passed = fixed + (places - fixed + rotation * (used - fixed)) % max(1, amount - fixed)
        return jnp.zeros((amount,), jnp.int32).at[order[jnp.where(places < fixed, places, passed)]].set(jnp.asarray(sizes, jnp.int32))

    sizes = jnp.where(number % 4 == 0, named(heavy_load, number // 4), named(common, number - number // 4 - 1))
    mixed = jax.random.permutation(jax.random.fold_in(own, 3), amount)
    source_of, receiver = mixed[0:amount // 2 * 2:2], mixed[1:amount // 2 * 2:2]
    margin = jnp.minimum(sizes[source_of] - 1, limit - sizes[receiver]) // 2
    margin = jnp.where((source_of == order[0]) | (receiver == order[0]) | (sizes[receiver] == 0), 0, jnp.maximum(margin, 0))
    passed = jax.random.randint(jax.random.fold_in(own, 4), (amount // 2,), 0, 1 << 20) % (margin + 1)
    sizes = sizes.at[source_of].add(-passed).at[receiver].add(passed)
    items = jnp.searchsorted(jnp.cumsum(sizes), jnp.arange(rows * top), side="right").astype(jnp.int32)
    listing = items.reshape(top, rows).T
    listing = listing[jax.random.permutation(jax.random.fold_in(own, 1), rows)]
    rotation = jax.random.randint(jax.random.fold_in(own, 2), (rows, 1), 0, top)
    return jnp.take_along_axis(listing, (jnp.arange(top)[None, :] + rotation) % top, axis=1)


def portions_of(number_of, total, bound, lean, full):
    loads = [(1 << 20) // math.isqrt(rank ** lean) + 1 for rank in range(1, number_of + 1)]
    largest = bound if full else min(bound, max(-(-total // number_of), total * loads[0] // sum(loads)))
    least = 1 if total - largest >= number_of - 1 else 0
    holding, surplus = [largest] + [least] * (number_of - 1), total - largest - least * (number_of - 1)
    while surplus > 0:
        free = [i for i in range(1, number_of) if holding[i] < largest] or [i for i in range(1, number_of) if holding[i] < bound]
        mass, remaining = sum([loads[i] for i in free]), surplus
        for i in free:
            addition = min(bound - holding[i], max(1, remaining * loads[i] // mass), surplus)
            holding[i] = holding[i] + addition
            surplus = surplus - addition
    return np.array(holding)


def centred(key, shape, deviation, reach, cuts=(), kind=jnp.bfloat16):
    factor_of = level_of(key, shape, cuts, -0.22, 0.18) if cuts else 1.0
    array = jax.random.normal(key, shape, jnp.float32) * deviation * factor_of
    return jnp.minimum(jnp.maximum(array, -reach), reach).astype(kind)


def bell_draw_with(key, dims, spread, limit, shards, heavy, kind=jnp.bfloat16):
    drawn = spread * jax.random.normal(key, dims, jnp.float32)
    if shards:
        drawn = drawn * level_of(key, dims, shards, -0.22, 0.18)
    return jnp.clip(strengthened(drawn, jax.random.fold_in(key, 3), *heavy), -limit, limit).astype(kind)


def setup_inputs(seed: int = 0) -> dict:
    splits = jax.random.split(jax.random.key(seed), 8)
    tokens = bell_draw_with(splits[0], (TOKENS, D), 1.0, 6.0, ((0, 32),), (0, 1, 32, 2.75))
    cotangent = centred(splits[1], (TOKENS, D), 0.25, 1.5, ((0, 32),))
    gates = jnp.clip(jnp.exp(math.log(1.0) - 1.6133518 * jax.random.uniform(splits[2], (TOKENS, TOP), jnp.float32) ** level_of(splits[2], (TOKENS, TOP), ((0, 32),), -0.2, 0.2)), 0.19921875, 1.0).astype(jnp.bfloat16)
    expert_ids_keys = jax.random.split(jax.random.fold_in(splits[3], 1), TOKENS // TOK_DEV)
    expert_ids_turns = jax.random.permutation(jax.random.fold_in(splits[3], 3), TOKENS // TOK_DEV)
    expert_ids = jax.vmap(lambda own, number: deal_out(jax.random.fold_in(splits[3], 2), own, number, TOK_DEV, EXPERTS, TOP, CAP, 2))(expert_ids_keys, expert_ids_turns).reshape((TOKENS, TOP))
    gate_w = centred(splits[4], (EXPERTS, D, H), D ** -0.5, 0.09375, ((0, 8),))
    up_w = centred(splits[5], (EXPERTS, D, H), D ** -0.5, 0.09375, ((0, 8),))
    down_w = centred(splits[6], (EXPERTS, H, D), H ** -0.5, 0.1875, ((0, 8),))
    return dict(tokens=tokens, cotangent=cotangent, gates=gates, expert_ids=expert_ids, gate_w=gate_w, up_w=up_w, down_w=down_w)


def reference(tokens, cotangent, gates, expert_ids, gate_w, up_w, down_w):
    slots_dev = TOK_DEV * TOP
    blocks = N_DP * N_EXPERT
    sentinel = TOKENS * TOP
    ids_block = expert_ids.reshape(blocks, slots_dev)
    onehot = (ids_block[:, :, None] == jnp.arange(EXPERTS, dtype=jnp.int32)[None, None, :]).astype(jnp.int32)
    position = jnp.sum(jnp.cumsum(onehot, axis=1) * onehot, axis=2) - 1
    block_id = jnp.arange(blocks, dtype=jnp.int32)[:, None]
    group_id = block_id // N_EXPERT
    source_id = block_id % N_EXPERT
    target = ((group_id * EXPERTS + ids_block) * N_EXPERT + source_id) * CAP + position
    flat_slot = jnp.arange(sentinel, dtype=jnp.int32).reshape(blocks, slots_dev)
    slot_map = jnp.full((N_DP * EXPERTS * N_EXPERT * CAP,), sentinel, jnp.int32)
    slot_map = slot_map.at[target.reshape(-1)].set(flat_slot.reshape(-1))
    slot_map = slot_map.reshape(N_DP, EXPERTS, N_EXPERT * CAP).transpose(1, 0, 2)
    tokens_ext = jnp.concatenate([tokens, jnp.zeros((1, D), tokens.dtype)], axis=0)
    cot_ext = jnp.concatenate([cotangent, jnp.zeros((1, D), cotangent.dtype)], axis=0)
    gates_ext = jnp.concatenate([gates.reshape(-1), jnp.zeros((1,), gates.dtype)], axis=0)

    def expert_step(running, inputs):
        slot_dx, slot_dg = running
        slot_index, gate_mat, up_mat, down_mat = inputs
        flat_index = slot_index.reshape(-1)
        row_token = jnp.where(flat_index == sentinel, TOKENS, flat_index // TOP)
        token_rows = tokens_ext[row_token]
        grad_rows = cot_ext[row_token]
        row_gates = gates_ext[flat_index].astype(jnp.float32)
        gate_pre = jnp.dot(token_rows, gate_mat, preferred_element_type=jnp.float32)
        up_pre = jnp.dot(token_rows, up_mat, preferred_element_type=jnp.float32)
        sigmoid_a = jax.nn.sigmoid(gate_pre)
        silu_a = gate_pre * sigmoid_a
        hidden = (silu_a * up_pre).astype(jnp.bfloat16)
        back = jnp.dot(grad_rows, down_mat.T, preferred_element_type=jnp.float32)
        gate_score = jnp.sum(back * hidden.astype(jnp.float32), axis=1).astype(jnp.bfloat16)
        hidden_grad = back * row_gates[:, None]
        gate_grad = (hidden_grad * up_pre * sigmoid_a * (1.0 + gate_pre * (1.0 - sigmoid_a))).astype(jnp.bfloat16)
        up_grad = (hidden_grad * silu_a).astype(jnp.bfloat16)
        row_grad = (jnp.dot(gate_grad, gate_mat.T, preferred_element_type=jnp.float32)
                    + jnp.dot(up_grad, up_mat.T, preferred_element_type=jnp.float32)).astype(jnp.bfloat16)
        grouped_x = token_rows.reshape(N_DP, -1, D).astype(jnp.float32)
        part_g = jnp.einsum('gmd,gmh->gdh', grouped_x, gate_grad.reshape(N_DP, -1, H).astype(jnp.float32))
        part_u = jnp.einsum('gmd,gmh->gdh', grouped_x, up_grad.reshape(N_DP, -1, H).astype(jnp.float32))
        part_g = lax.optimization_barrier(part_g.astype(jnp.bfloat16)).astype(jnp.float32)
        part_u = lax.optimization_barrier(part_u.astype(jnp.bfloat16)).astype(jnp.float32)
        grad_g = (jnp.sum(part_g, axis=0) * (1.0 / N_DP)).astype(jnp.bfloat16)
        grad_u = (jnp.sum(part_u, axis=0) * (1.0 / N_DP)).astype(jnp.bfloat16)
        slot_dx = slot_dx.at[flat_index].set(row_grad)
        slot_dg = slot_dg.at[flat_index].set(gate_score)
        return (slot_dx, slot_dg), (grad_g, grad_u)

    start_dx = jnp.zeros((sentinel + 1, D), jnp.bfloat16)
    start_dg = jnp.zeros((sentinel + 1,), jnp.bfloat16)
    (slot_dx, slot_dg), (grad_gate_w, grad_up_w) = lax.scan(
        expert_step, (start_dx, start_dg), (slot_map, gate_w, up_w, down_w))
    grad_tokens = jnp.sum(slot_dx[:sentinel].reshape(TOKENS, TOP, D).astype(jnp.float32), axis=1).astype(jnp.bfloat16)
    grad_gates = slot_dg[:sentinel].reshape(TOKENS, TOP)
    return (grad_tokens, grad_gate_w, grad_up_w, grad_gates)
```

```python
import functools

import jax
import jax.numpy as jnp
from jax import lax
from jax.experimental import pallas as pl
from jax.experimental.pallas import tpu as pltpu
from jax.sharding import PartitionSpec as P

F32 = jnp.float32
BF16 = jnp.bfloat16
NT = (((1,), (1,)), ((), ()))
TN = (((0,), (0,)), ((), ()))


def params(mib=48):
    return pltpu.CompilerParams(vmem_limit_bytes=mib << 20)


def cost(flops, nbytes):
    return pl.CostEstimate(flops=int(flops), bytes_accessed=int(nbytes), transcendentals=0)


def vmem(count):
    return [pl.BlockSpec(memory_space=pltpu.VMEM)] * count


def smem():
    return pl.BlockSpec(memory_space=pltpu.SMEM)


def prep_kernel(n, cap, me_ref, ids_ref, gates_ref, tok_ref, meta_ref, *out_refs):
    toks = tok_ref.shape[0]
    expert = lax.broadcasted_iota(jnp.int32, (n, toks), 0) ^ me_ref[0]
    first = ids_ref[0:1, :] == expert
    second = ids_ref[1:2, :] == expert
    count = (first | second).astype(F32)
    before = (
        lax.broadcasted_iota(jnp.int32, (toks, toks), 0)
        < lax.broadcasted_iota(jnp.int32, (toks, toks), 1)
    ).astype(F32)
    position = jnp.dot(count.astype(BF16), before.astype(BF16), preferred_element_type=F32)
    code = jnp.where(first | second, position, -1.0)
    gates = gates_ref[...].astype(F32)
    weight = jnp.where(first, gates[0:1, :], 0.0) + jnp.where(second, gates[1:2, :], 0.0)
    meta_ref[...] = jnp.concatenate([code, weight], axis=0).astype(BF16)
    select_rows(n, cap, code, tok_ref, out_refs)


def select_rows(n, cap, code, tok_ref, out_refs):
    toks = tok_ref.shape[0]
    slot = lax.broadcasted_iota(jnp.int32, (cap, toks), 0).astype(F32)
    for j in range(n):
        pick = (slot == code[j : j + 1, :]).astype(F32).astype(BF16)
        out_refs[j][...] = jnp.dot(pick, tok_ref[...], preferred_element_type=F32).astype(BF16)


def select_kernel(n, cap, meta_ref, tok_ref, *out_refs):
    code = meta_ref[...].astype(F32)[0:n, :]
    select_rows(n, cap, code, tok_ref, out_refs)


def forward_kernel(n, cap, *refs):
    x_refs, meta_refs = refs[:n], refs[n : 2 * n]
    gate_ref, up_ref, rows_ref, hidden_ref, pa_ref, pb_ref, w_ref = refs[2 * n :]
    toks = meta_refs[0].shape[1]

    @pl.when(pl.program_id(0) == 0)
    def _():
        slot = lax.broadcasted_iota(jnp.int32, (cap, toks), 0).astype(F32)
        for j in range(n):
            rows_ref[j * cap : (j + 1) * cap, :] = x_refs[j][...]
            meta = meta_refs[j][...].astype(F32)
            picked = jnp.where(slot == meta[j : j + 1, :], meta[n + j : n + j + 1, :], 0.0)
            total = jnp.sum(picked, axis=1, keepdims=True)
            w_ref[j * cap : (j + 1) * cap, :] = jnp.broadcast_to(total, (cap, w_ref.shape[1]))

    a = jnp.dot(rows_ref[...], gate_ref[0], preferred_element_type=F32)
    b = jnp.dot(rows_ref[...], up_ref[0], preferred_element_type=F32)
    w = w_ref[:, 0:1]
    sig = jax.nn.sigmoid(a)
    silu = a * sig
    hidden_ref[...] = (silu * b).astype(BF16)
    pa_ref[...] = w * b * sig * (1.0 + a * (1.0 - sig))
    pb_ref[...] = w * silu


def back_kernel(n, cap, *refs):
    y_refs = refs[:n]
    hidden_ref, pa_ref, pb_ref, down_ref, grads_ref, score_ref, rows_ref, part_ref = refs[n:]
    step = pl.program_id(0)

    @pl.when(step == 0)
    def _():
        for j in range(n):
            rows_ref[j * cap : (j + 1) * cap, :] = y_refs[j][...]
        part_ref[...] = jnp.zeros_like(part_ref)

    back = lax.dot_general(rows_ref[...], down_ref[0], NT, preferred_element_type=F32)
    grads_ref[0] = (back * pa_ref[...]).astype(BF16)
    grads_ref[1] = (back * pb_ref[...]).astype(BF16)
    prod = back * hidden_ref[...].astype(F32)
    part = part_ref[...]
    for c in range(prod.shape[1] // 128):
        part = part + prod[:, c * 128 : (c + 1) * 128]
    part_ref[...] = part

    @pl.when(step == pl.num_programs(0) - 1)
    def _():
        total = jnp.sum(jnp.transpose(part_ref[...]), axis=0, keepdims=True)
        shape = score_ref.shape
        top = lax.broadcasted_iota(jnp.int32, shape, 0) == 0
        score_ref[...] = jnp.where(top, jnp.broadcast_to(total, shape), 0.0).astype(BF16)


def rowgrad_kernel(count, feats, me_ref, grads_ref, score_ref, gate_ref, up_ref, *out_refs):
    del me_ref
    val = lax.dot_general(gate_ref[0], grads_ref[0], NT, preferred_element_type=F32)
    val = val + lax.dot_general(up_ref[0], grads_ref[1], NT, preferred_element_type=F32)
    val = val.astype(BF16)
    for i in range(count):

        @pl.when(pl.program_id(0) == i)
        def _():
            out_refs[i][0:feats, :] = val
            out_refs[i][feats:, :] = score_ref[...]


def combine_kernel(n, cap, feats, me_ref, ids_ref, *refs):
    meta_refs, got_refs = refs[:n], refs[n : 2 * n]
    out_ref, gates_ref = refs[2 * n :]
    me = me_ref[0]
    rows = n * cap
    toks = meta_refs[0].shape[1]
    metas = [meta_refs[j][...].astype(F32) for j in range(n)]
    total = jnp.zeros((feats, n * toks), F32)
    gg0 = jnp.zeros((16, toks), F32)
    gg1 = jnp.zeros((16, toks), F32)
    row = lax.broadcasted_iota(jnp.int32, (rows, n * toks), 0).astype(F32)
    for k in range(n):
        wanted = []
        for j in range(n):
            code = metas[j][j ^ k : (j ^ k) + 1, :]
            wanted.append(jnp.where(code >= 0.0, code + float((j ^ k) * cap), -1.0))
        wanted = jnp.concatenate(wanted, axis=1)
        pick = (row == wanted).astype(F32).astype(BF16)
        total = total + jnp.dot(got_refs[k][0:feats, :], pick, preferred_element_type=F32)
        score = jnp.dot(got_refs[k][feats:, :], pick[:, 0:toks], preferred_element_type=F32)
        gg0 = gg0 + jnp.where(ids_ref[0:1, :] == (me ^ k), score, 0.0)
        gg1 = gg1 + jnp.where(ids_ref[1:2, :] == (me ^ k), score, 0.0)
    for j in range(n):
        place = pl.multiple_of((me ^ j) * toks, toks)
        out_ref[:, pl.ds(place, toks)] = total[:, j * toks : (j + 1) * toks].astype(BF16)
    gates_ref[...] = jnp.concatenate([gg0[0:1], gg1[0:1]], axis=0).astype(BF16)


def weights_kernel(ndp, *refs):
    x_refs, g_refs = refs[:ndp], refs[ndp : 2 * ndp]
    gate_ref, up_ref = refs[2 * ndp :]
    for half, out in ((0, gate_ref), (1, up_ref)):
        total = None
        for q in range(ndp):
            term = lax.dot_general(x_refs[q][...], g_refs[q][half], TN, preferred_element_type=F32)
            total = term if total is None else total + term
        out[0] = (total * (1.0 / ndp)).astype(BF16)


def local(tokens, cotangent, gates, expert_ids, gate_w, up_w, down_w):
    toks, d = tokens.shape
    top = expert_ids.shape[1]
    h = gate_w.shape[2]
    n = lax.axis_size("expert")
    ndp = lax.axis_size("dp")
    cap = -(-(3 * toks * top // (2 * n)) // 16) * 16
    rows = n * cap
    feats = d // n
    block = d // ndp
    me = lax.axis_index("expert").astype(jnp.int32)
    my_dp = lax.axis_index("dp")
    me_arr = me.reshape(1)
    ids_t = expert_ids.T
    gates_t = gates.T

    def swap(v, k):
        return lax.ppermute(v, "expert", [(i, i ^ k) for i in range(n)])

    def swap_dp(v, q):
        return lax.ppermute(v, "dp", [(i, i ^ q) for i in range(ndp)])

    block_shape = jax.ShapeDtypeStruct((cap, d), BF16)
    meta, *send_x = pl.pallas_call(
        functools.partial(prep_kernel, n, cap),
        out_shape=[jax.ShapeDtypeStruct((2 * n, toks), BF16)] + [block_shape] * n,
        in_specs=[smem()] + vmem(3),
        out_specs=vmem(n + 1),
        compiler_params=params(),
        cost_estimate=cost(2 * rows * toks * d, 2 * (rows + toks) * d),
        name="prep",
    )(me_arr, ids_t, gates_t, tokens)
    metas = [meta] + [swap(meta, k) for k in range(1, n)]
    got_x = [send_x[0]] + [swap(send_x[k], k) for k in range(1, n)]

    send_y = pl.pallas_call(
        functools.partial(select_kernel, n, cap),
        out_shape=[block_shape] * n,
        in_specs=vmem(2),
        out_specs=vmem(n),
        compiler_params=params(),
        cost_estimate=cost(2 * rows * toks * d, 2 * (rows + toks) * d),
        name="select",
    )(meta, cotangent)
    got_y = [send_y[0]] + [swap(send_y[k], k) for k in range(1, n)]

    tile = 256
    steps = h // tile
    whole = lambda shape: pl.BlockSpec(shape, lambda i: (0,) * len(shape))
    x_rows, hidden, pa, pb = pl.pallas_call(
        functools.partial(forward_kernel, n, cap),
        grid=(steps,),
        out_shape=[
            jax.ShapeDtypeStruct((rows, d), BF16),
            jax.ShapeDtypeStruct((rows, h), BF16),
            jax.ShapeDtypeStruct((rows, h), F32),
            jax.ShapeDtypeStruct((rows, h), F32),
        ],
        in_specs=[whole((cap, d))] * n
        + [whole((2 * n, toks))] * n
        + [pl.BlockSpec((1, d, tile), lambda i: (0, 0, i))] * 2,
        out_specs=[whole((rows, d))] + [pl.BlockSpec((rows, tile), lambda i: (0, i))] * 3,
        scratch_shapes=[pltpu.VMEM((rows, 128), F32)],
        compiler_params=params(),
        cost_estimate=cost(4 * rows * d * h, 4 * d * h + 4 * rows * d + 10 * rows * h),
        name="forward",
    )(*got_x, *metas, gate_w, up_w)

    def block_of(q):
        return lax.dynamic_slice_in_dim(x_rows, (my_dp ^ q) * block, block, axis=1)

    x_parts = [block_of(0)] + [swap_dp(block_of(q), q) for q in range(1, ndp)]

    grads, score = pl.pallas_call(
        functools.partial(back_kernel, n, cap),
        grid=(steps,),
        out_shape=[
            jax.ShapeDtypeStruct((2, rows, h), BF16),
            jax.ShapeDtypeStruct((16, rows), BF16),
        ],
        in_specs=[whole((cap, d))] * n
        + [pl.BlockSpec((rows, tile), lambda i: (0, i))] * 3
        + [pl.BlockSpec((1, tile, d), lambda i: (0, i, 0))],
        out_specs=[pl.BlockSpec((2, rows, tile), lambda i: (0, 0, i)), whole((16, rows))],
        scratch_shapes=[pltpu.VMEM((rows, d), BF16), pltpu.VMEM((rows, 128), F32)],
        compiler_params=params(),
        cost_estimate=cost(2 * rows * d * h, 2 * d * h + 2 * rows * d + 14 * rows * h),
        name="back",
    )(*got_y, hidden, pa, pb, down_w)

    def rowgrads(parts):
        first, count = parts[0], len(parts)
        spec = pl.BlockSpec((1, feats, h), lambda i, me_ref: (0, me_ref[0] ^ (first - i), 0))
        fixed = lambda shape: pl.BlockSpec(shape, lambda i, me_ref: (0,) * len(shape))
        return pl.pallas_call(
            functools.partial(rowgrad_kernel, count, feats),
            grid_spec=pltpu.PrefetchScalarGridSpec(
                num_scalar_prefetch=1,
                grid=(count,),
                in_specs=[fixed((2, rows, h)), fixed((16, rows)), spec, spec],
                out_specs=[fixed((feats + 16, rows))] * count,
            ),
            out_shape=[jax.ShapeDtypeStruct((feats + 16, rows), BF16)] * count,
            compiler_params=params(),
            cost_estimate=cost(4 * count * feats * rows * h, 4 * count * feats * h + 4 * rows * h),
            name="rowgrad",
        )(me_arr, grads, score, gate_w, up_w)

    order = list(range(n - 1, -1, -1))
    half = n // 2
    back_rows = [None] * n
    for parts in (order[: half // 2], order[half // 2 : half], order[half:]):
        for k, sent in zip(parts, rowgrads(parts)):
            back_rows[k] = swap(sent, k) if k else sent

    g_parts = [grads] + [None] * (ndp - 1)
    for q in range(0, ndp, 2):
        if q:
            g_parts[q] = swap_dp(grads, q)
        g_parts[q + 1] = swap_dp(g_parts[q], 1)

    tile_w = 256
    out_spec = pl.BlockSpec((1, block, tile_w), lambda i: (0, 0, i))
    grad_gate_w, grad_up_w = pl.pallas_call(
        functools.partial(weights_kernel, ndp),
        grid=(h // tile_w,),
        out_shape=[jax.ShapeDtypeStruct((1, block, h), BF16)] * 2,
        in_specs=[whole((rows, block))] * ndp
        + [pl.BlockSpec((2, rows, tile_w), lambda i: (0, 0, i))] * ndp,
        out_specs=[out_spec, out_spec],
        compiler_params=params(),
        cost_estimate=cost(
            4 * ndp * rows * block * h, 2 * ndp * rows * (block + 2 * h) + 4 * block * h
        ),
        name="weights",
    )(*x_parts, *g_parts)

    summed, gg = pl.pallas_call(
        functools.partial(combine_kernel, n, cap, feats),
        out_shape=[
            jax.ShapeDtypeStruct((feats, n * toks), BF16),
            jax.ShapeDtypeStruct((2, toks), BF16),
        ],
        in_specs=[smem()] + vmem(1 + 2 * n),
        out_specs=vmem(2),
        compiler_params=params(),
        cost_estimate=cost(2 * n * feats * rows * n * toks, 2 * feats * n * (rows + toks)),
        name="combine",
    )(me_arr, ids_t, *metas, *back_rows)
    return summed.T, grad_gate_w, grad_up_w, gg.T


def solution(mesh):
    placed = (
        P(("dp", "expert"), None),
        P(("dp", "expert"), None),
        P(("dp", "expert"), None),
        P(("dp", "expert"), None),
        P("expert", None, None),
        P("expert", None, None),
        P("expert", None, None),
    )
    return jax.shard_map(
        local,
        mesh=mesh,
        in_specs=placed,
        out_specs=(
            P("dp", "expert"),
            P("expert", "dp", None),
            P("expert", "dp", None),
            P(("dp", "expert"), None),
        ),
        check_vma=False,
    )
```

```python
import functools

import jax
import jax.numpy as jnp
from jax import lax
from jax.experimental import pallas as pl
from jax.experimental.pallas import tpu as pltpu
from jax.sharding import PartitionSpec as P

F32 = jnp.float32
BF16 = jnp.bfloat16
NT = (((1,), (1,)), ((), ()))
TN = (((0,), (0,)), ((), ()))


def params(mib=48):
    return pltpu.CompilerParams(vmem_limit_bytes=mib << 20)


def vmem(count):
    return [pl.BlockSpec(memory_space=pltpu.VMEM)] * count


def smem():
    return pl.BlockSpec(memory_space=pltpu.SMEM)


LONG = 1 << 40


def pick_rows(cap, code, meta, tok_ref, dest):
    toks, d = tok_ref.shape
    slot = lax.broadcasted_iota(jnp.int32, (cap, toks), 0).astype(F32)
    for j, ref, at in dest:
        pick = (slot == code[j : j + 1, :]).astype(F32).astype(BF16)
        chosen = jnp.dot(pick, tok_ref[...], preferred_element_type=F32).astype(BF16)
        ref[at : at + cap, 0:d] = chosen
        if ref.shape[1] > d:
            ref[at : at + cap, d:] = jnp.zeros((cap, toks), BF16)
            ref[at : at + meta.shape[0], d:] = meta


def prep_kernel(n, nx, cap, me_ref, ids_ref, gates_ref, tok_ref, cot_ref, meta_ref, *out_refs):
    toks = tok_ref.shape[0]
    nz = n // nx
    expert = lax.broadcasted_iota(jnp.int32, (n, toks), 0) ^ me_ref[0]
    first = ids_ref[0:1, :] == expert
    second = ids_ref[1:2, :] == expert
    count = (first | second).astype(F32)
    before = (
        lax.broadcasted_iota(jnp.int32, (toks, toks), 0)
        < lax.broadcasted_iota(jnp.int32, (toks, toks), 1)
    ).astype(F32)
    position = jnp.dot(count.astype(BF16), before.astype(BF16), preferred_element_type=F32)
    code = jnp.where(first | second, position, -1.0)
    gates = gates_ref[...].astype(F32)
    weight = jnp.where(first, gates[0:1, :], 0.0) + jnp.where(second, gates[1:2, :], 0.0)
    meta = jnp.concatenate([code, weight], axis=0).astype(BF16)
    meta_ref[...] = meta
    near_refs, rest, y_refs = out_refs[: nz - 2], out_refs[nz - 2 : 1 - nx], out_refs[1 - nx :]
    near = [(zk * nx + xo, near_refs[zk - 1], xo * cap) for zk in range(1, nz - 1) for xo in range(nx)]
    spots = list(range(n - nx, n)) + list(range(nx))
    pick_rows(cap, code, meta, tok_ref, near + [(j, ref, 0) for j, ref in zip(spots, rest)])
    by_column = [(zk * nx + xo, y_refs[xo - 1], zk * cap) for zk in range(nz) for xo in range(1, nx)]
    pick_rows(cap, code, meta, cot_ref, by_column)


def second_kernel(n, nx, cap, meta_ref, cot_ref, *refs):
    nz = n // nx
    y_came, x_own, x_came = refs[: nx - 1], refs[nx - 1 : 2 * nx - 2], refs[2 * nx - 2 : 2 * nx + nz - 4]
    y_refs, x_refs = refs[1 - nx - nz : 1 - nx], refs[1 - nx :]
    meta = meta_ref[...]
    own = [(zk * nx, y_refs[zk], 0) for zk in range(nz)]
    pick_rows(cap, meta.astype(F32)[0:n, :], meta, cot_ref, own)
    for xo in range(1, nx):
        for zk in range(1, nz):
            y_refs[zk][xo * cap : (xo + 1) * cap, :] = y_came[xo - 1][zk * cap : (zk + 1) * cap, :]
        x_refs[xo - 1][0:cap, :] = x_own[xo - 1][...]
        for i, ref in enumerate(x_came, 1):
            x_refs[xo - 1][i * cap : (i + 1) * cap, :] = ref[xo * cap : (xo + 1) * cap, :]


def found_x(n, nx, cap, refs):
    nz = n // nx
    z_refs, side_refs, far_refs = refs[: nz - 1], refs[nz - 1 : nz + nx - 2], refs[nz + nx - 2 :]
    found = []
    for zk in range(nz - 1):
        found += [(z_refs[zk], 0)] + [(side_refs[xo], zk * cap) for xo in range(nx - 1)]
    return found + [(ref, 0) for ref in far_refs]


def found_y(n, nx, cap, refs):
    nz = n // nx
    z_refs, y_refs = refs[:nz], refs[nz:]
    return [
        (z_refs[zk], xo * cap) if zk or not xo else (y_refs[xo - 1], 0)
        for zk in range(nz)
        for xo in range(nx)
    ]


def fence_kernel(out_ref):
    out_ref[...] = jnp.zeros_like(out_ref)


def forward_kernel(n, nx, cap, count, ny, place_ref, *refs):
    found = found_x(n, nx, cap, refs[:count])
    meta_ref, gate_ref, up_ref, pass_ref, *out_refs = refs[count:]
    part_refs, out_refs = out_refs[:ny], out_refs[ny:]
    hidden_ref, pa_ref, pb_ref, passed_ref, metas_ref, w_ref, rows_ref = out_refs
    toks = meta_ref.shape[1]
    d = rows_ref.shape[1]
    width = part_refs[0].shape[1]

    @pl.when(pl.program_id(0) == 0)
    def _():
        slot = lax.broadcasted_iota(jnp.int32, (cap, toks), 0).astype(F32)
        for j, (ref, at) in enumerate(found):
            rows_ref[j * cap : (j + 1) * cap, :] = ref[at : at + cap, 0:d]
            if j:
                metas_ref[j] = ref[at : at + 2 * n, d:]
            else:
                metas_ref[j] = meta_ref[...]
            meta = metas_ref[j].astype(F32)
            picked = jnp.where(slot == meta[j : j + 1, :], meta[n + j : n + j + 1, :], 0.0)
            total = jnp.sum(picked, axis=1, keepdims=True)
            w_ref[j * cap : (j + 1) * cap, :] = jnp.broadcast_to(total, (cap, w_ref.shape[1]))
        for yo, ref in enumerate(part_refs):
            at = pl.multiple_of((place_ref[0] ^ yo) * width, 128)
            ref[...] = rows_ref[:, pl.ds(at, width)]
        passed_ref[...] = pass_ref[...]

    a = jnp.dot(rows_ref[...], gate_ref[0], preferred_element_type=F32)
    b = jnp.dot(rows_ref[...], up_ref[0], preferred_element_type=F32)
    w = w_ref[:, 0:1]
    sig = jax.nn.sigmoid(a)
    silu = a * sig
    hidden_ref[...] = (silu * b).astype(BF16)
    pa_ref[...] = w * b * sig * (1.0 + a * (1.0 - sig))
    pb_ref[...] = w * silu


def back_kernel(n, nx, cap, count, *refs):
    found = found_y(n, nx, cap, refs[:count])
    hidden_ref, pa_ref, pb_ref, down_ref, grads_ref, score_ref, rows_ref, part_ref = refs[count:]
    step = pl.program_id(0)

    @pl.when(step == 0)
    def _():
        for j, (ref, at) in enumerate(found):
            rows_ref[j * cap : (j + 1) * cap, :] = ref[at : at + cap, :]
        part_ref[...] = jnp.zeros_like(part_ref)

    back = lax.dot_general(rows_ref[...], down_ref[0], NT, preferred_element_type=F32)
    grads_ref[0] = (back * pa_ref[...]).astype(BF16)
    grads_ref[1] = (back * pb_ref[...]).astype(BF16)
    prod = back * hidden_ref[...].astype(F32)
    part = part_ref[...]
    for c in range(prod.shape[1] // 128):
        part = part + prod[:, c * 128 : (c + 1) * 128]
    part_ref[...] = part

    @pl.when(step == pl.num_programs(0) - 1)
    def _():
        total = jnp.sum(jnp.transpose(part_ref[...]), axis=0, keepdims=True)
        shape = score_ref.shape
        top = lax.broadcasted_iota(jnp.int32, shape, 0) == 0
        score_ref[...] = jnp.where(top, jnp.broadcast_to(total, shape), 0.0).astype(BF16)


def rowgrad_kernel(places, dest_ref, grads_ref, score_ref, gate_ref, up_ref, *out_refs):
    del dest_ref
    size = gate_ref.shape[1]
    val = lax.dot_general(gate_ref[0], grads_ref[0], NT, preferred_element_type=F32)
    val = val + lax.dot_general(up_ref[0], grads_ref[1], NT, preferred_element_type=F32)
    val = val.astype(BF16)
    for i, (out, at) in enumerate(places):

        @pl.when(pl.program_id(0) == i)
        def _():
            out_refs[out][at : at + size, :] = val
            out_refs[out][at + size : at + size + 16, :] = score_ref[...]


def second_back_kernel(nx, size, came_ref, *refs):
    for i in range(nx - 1):
        out = refs[nx - 1 + i]
        out[0:size, :] = refs[i][...]
        out[size:, :] = came_ref[(i + 1) * size : (i + 2) * size, :]


def combine_kernel(n, cap, feats, parts, last, me_ref, ids_ref, metas_ref, *refs):
    me = me_ref[0]
    rows = n * cap
    toks = metas_ref.shape[2]
    metas = [metas_ref[j].astype(F32) for j in range(n)]
    if last:
        total_ref, part_ref, out_ref, gates_ref = refs[-4:]
        total = total_ref[...]
        gg = [part_ref[0], part_ref[1]]
    else:
        total_ref, part_ref = refs[-2:]
        total = jnp.zeros((feats, n * toks), F32)
        gg = [jnp.zeros((16, toks), F32)] * 2
    row = lax.broadcasted_iota(jnp.int32, (rows, n * toks), 0).astype(F32)
    for k, which, at in parts:
        wanted = []
        for j in range(n):
            code = metas[j][j ^ k : (j ^ k) + 1, :]
            wanted.append(jnp.where(code >= 0.0, code + float((j ^ k) * cap), -1.0))
        wanted = jnp.concatenate(wanted, axis=1)
        pick = (row == wanted).astype(F32).astype(BF16)
        got = refs[which][at : at + feats, :]
        total = total + jnp.dot(got, pick, preferred_element_type=F32)
        got = refs[which][at + feats : at + feats + 16, :]
        score = jnp.dot(got, pick[:, 0:toks], preferred_element_type=F32)
        gg = [gg[c] + jnp.where(ids_ref[c : c + 1, :] == (me ^ k), score, 0.0) for c in (0, 1)]
    if not last:
        total_ref[...] = total
        part_ref[0] = gg[0]
        part_ref[1] = gg[1]
        return
    for j in range(n):
        place = pl.multiple_of((me ^ j) * toks, toks)
        out_ref[:, pl.ds(place, toks)] = total[:, j * toks : (j + 1) * toks].astype(BF16)
    gates_ref[...] = jnp.concatenate([gg[0][0:1], gg[1][0:1]], axis=0).astype(BF16)


def stack_kernel(ny, core_ref, *refs):
    g_refs, x_refs = refs[:ny], refs[ny : 2 * ny]
    stack_ref, keep_ref, send_ref = refs[2 * ny :]
    block = keep_ref.shape[2]
    for yo in range(ny):
        stack_ref[yo] = g_refs[yo][...]

        @pl.when(core_ref[0] == 0)
        def _():
            keep_ref[yo] = x_refs[yo][:, :block]
            send_ref[yo] = x_refs[yo][:, block:]

        @pl.when(core_ref[0] != 0)
        def _():
            keep_ref[yo] = x_refs[yo][:, block:]
            send_ref[yo] = x_refs[yo][:, :block]


def weights_kernel(ndp, *refs):
    ny = ndp // 2
    x_refs, g_refs, stack_ref = refs[:2], refs[2 : 2 + ny], refs[2 + ny]
    gate_ref, up_ref = refs[-2:]
    for half, out in ((0, gate_ref), (1, up_ref)):
        total = None
        for q in range(ndp):
            g = stack_ref[q // 2, half] if q % 2 else g_refs[q // 2][half]
            term = lax.dot_general(x_refs[q % 2][q // 2], g, TN, preferred_element_type=F32)
            total = term if total is None else total + term
        out[0] = (total * (1.0 / ndp)).astype(BF16)


def local(tokens, cotangent, gates, expert_ids, gate_w, up_w, down_w):
    toks, d = tokens.shape
    top = expert_ids.shape[1]
    h = gate_w.shape[2]
    n = lax.axis_size("expert")
    ndp = lax.axis_size("dp")
    nz = 4
    nx = n // nz
    ny = ndp // 2
    cap = -(-(3 * toks * top // (2 * n)) // 16) * 16
    rows = n * cap
    feats = d // n
    size = feats + 16
    block = d // ndp
    wide = d + toks
    me = lax.axis_index("expert").astype(jnp.int32)
    my_dp = lax.axis_index("dp").astype(jnp.int32)
    me_arr = me.reshape(1)
    my_y, my_core = (my_dp // 2).reshape(1), (my_dp % 2).reshape(1)
    ids_t = expert_ids.T
    gates_t = gates.T
    any_space = pl.BlockSpec(memory_space=pl.ANY)

    def swap(v, k):
        return lax.ppermute(v, "expert", [(i, i ^ k) for i in range(n)])

    def swap_dp(v, q):
        return lax.ppermute(v, "dp", [(i, i ^ q) for i in range(ndp)])

    def shape(*dims, dtype=BF16):
        return jax.ShapeDtypeStruct(dims, dtype)

    previous = []

    def run(body, name, outs, args, in_specs, out_specs, after=(), grid=(), scalars=0, scratch=(), weight=LONG):
        waits = [*after, *previous]
        first = len(args)

        def trimmed(*refs):
            body(*refs[:first], *refs[first + len(waits) :])

        made = pl.pallas_call(
            trimmed,
            grid_spec=pltpu.PrefetchScalarGridSpec(
                num_scalar_prefetch=scalars,
                grid=grid,
                in_specs=[*in_specs, *[any_space] * len(waits)],
                out_specs=out_specs,
                scratch_shapes=scratch,
            ),
            out_shape=outs,
            compiler_params=params(),
            cost_estimate=pl.CostEstimate(flops=weight, bytes_accessed=weight, transcendentals=0),
            name=name,
        )(*args, *waits)
        previous[:] = made[-1:]
        return made

    def call(body, name, outs, args, after=(), scalars=0):
        in_specs = [smem()] * scalars + vmem(len(args) - scalars)
        return run(body, name, outs, args, in_specs, vmem(len(outs)), after)

    def fence(after):
        call(fence_kernel, "fence", [shape(8, 128, dtype=F32)], [], after)

    near_z = range(1, nz - 1)
    meta, *made = call(
        functools.partial(prep_kernel, n, nx, cap),
        "prep",
        [shape(2 * n, toks)]
        + [shape(nx * cap, wide)] * (nz - 2)
        + [shape(cap, wide)] * nx
        + [shape(cap, d)]
        + [shape(cap, wide)] * (nx - 1)
        + [shape(nz * cap, d)] * (nx - 1),
        [me_arr, ids_t, gates_t, tokens, cotangent],
        scalars=1,
    )
    x_near, x_far, made = made[: nz - 2], made[nz - 2 : nz - 2 + nx], made[nz - 2 + nx :]
    x_own, x_side, y_side = made[0], made[1:nx], made[nx:]
    x_near = [swap(v, zk * nx) for zk, v in zip(near_z, x_near)]
    x_far = [swap(v, n - nx + xo) for xo, v in enumerate(x_far)]
    y_side = [swap(v, xo) for xo, v in enumerate(y_side, 1)]
    made = call(
        functools.partial(second_kernel, n, nx, cap),
        "second",
        [shape(cap, d)]
        + [shape(nx * cap, d)] * (nz - 1)
        + [shape((nz - 1) * cap, wide)] * (nx - 1),
        [meta, cotangent, *y_side, *x_side, *x_near],
    )
    y_own, y_late = made[0], made[1]
    x_side = [swap(v, xo) for xo, v in enumerate(made[nz:], 1)]
    y_z = [swap(made[zk], zk * nx) for zk in range(2, nz)]
    got_x = [x_own, *x_near, *x_side, *x_far]
    fence(x_far)

    tile = 256
    steps = h // tile
    whole = lambda shape: pl.BlockSpec(shape, lambda i: (0,) * len(shape))
    column = pl.BlockSpec((rows, tile), lambda i: (0, i))
    *x_parts, hidden, pa, pb, y_late, metas = run(
        functools.partial(forward_kernel, n, nx, cap, len(got_x), ny),
        "forward",
        [shape(rows, 2 * block)] * ny
        + [shape(rows, h), shape(rows, h, dtype=F32), shape(rows, h, dtype=F32)]
        + [shape(nx * cap, d), shape(n, 2 * n, toks)],
        [my_y, *got_x, meta, gate_w, up_w, y_late],
        [smem()]
        + [whole(v.shape) for v in got_x]
        + [whole((2 * n, toks))]
        + [pl.BlockSpec((1, d, tile), lambda i: (0, 0, i))] * 2
        + [whole((nx * cap, d))],
        [whole((rows, 2 * block))] * ny
        + [column] * 3
        + [whole((nx * cap, d)), whole((n, 2 * n, toks))],
        grid=(steps,),
        scratch=[pltpu.VMEM((rows, 128), F32), pltpu.VMEM((rows, d), BF16)],
        weight=1,
    )
    x_parts = [x_parts[0]] + [swap_dp(v, 2 * yo) for yo, v in enumerate(x_parts[1:], 1)]
    y_late = swap(y_late, nx)
    fence(y_z)
    got_y = [y_own, y_late, *y_z, *y_side]

    grads, score = run(
        functools.partial(back_kernel, n, nx, cap, len(got_y)),
        "back",
        [shape(2, rows, h), shape(16, rows)],
        [*got_y, hidden, pa, pb, down_w],
        [whole(v.shape) for v in got_y]
        + [column] * 3
        + [pl.BlockSpec((1, tile, d), lambda i: (0, i, 0))],
        [pl.BlockSpec((2, rows, tile), lambda i: (0, 0, i)), whole((16, rows))],
        grid=(steps,),
        scratch=[pltpu.VMEM((rows, d), BF16), pltpu.VMEM((rows, 128), F32)],
        weight=1,
    )
    g_parts = [grads] + [swap_dp(grads, 2 * yo) for yo in range(1, ny)]

    def rowgrads(places, outs, after=(), weight=1):
        dest = jnp.array([k for k, _, _ in places], jnp.int32) ^ me
        spec = pl.BlockSpec((1, feats, h), lambda i, dest_ref: (0, dest_ref[i], 0))
        fixed = lambda dims: pl.BlockSpec(dims, lambda i, dest_ref: (0,) * len(dims))
        return run(
            functools.partial(rowgrad_kernel, [(out, at) for _, out, at in places]),
            "rowgrad",
            [shape(size * many, rows) for many in outs],
            [dest, grads, score, gate_w, up_w],
            [fixed((2, rows, h)), fixed((16, rows)), spec, spec],
            [fixed((size * many, rows)) for many in outs],
            after,
            grid=(len(places),),
            scalars=1,
            weight=weight,
        )

    far = list(range(n - nx, n))
    mids = list(range(2 * nx, n - nx))
    now, held = mids[len(mids) // 2 :], mids[: len(mids) // 2]
    sent = rowgrads([(k, i, 0) for i, k in enumerate(far)], [1] * nx)
    early = [swap(v, k) for k, v in zip(far, sent)]
    *sent, near = rowgrads(
        [(k, i, 0) for i, k in enumerate(now)]
        + [(nx + xo, len(now), xo * size) for xo in range(nx)],
        [1] * len(now) + [nx],
        x_parts[1:],
    )
    near = swap(near, nx)
    middle = [swap(v, k) for k, v in zip(now, sent)]
    own, *sent = rowgrads(
        [(k, i, 0) for i, k in enumerate([0, *range(1, nx), *held])],
        [1] * (nx + len(held)),
        weight=LONG,
    )
    late = [swap(v, k) for k, v in zip(held, sent[nx - 1 :])]
    g_stack, x_keep, x_send = call(
        functools.partial(stack_kernel, ny),
        "stack",
        [shape(ny, 2, rows, h)] + [shape(ny, rows, block)] * 2,
        [my_core, *g_parts, *x_parts],
        early,
        scalars=1,
    )
    g_stack, x_came = swap_dp(g_stack, 1), swap_dp(x_send, 1)

    sent = call(
        functools.partial(second_back_kernel, nx, size),
        "second_back",
        [shape(2 * size, rows)] * (nx - 1),
        [near, *sent[: nx - 1]],
    )
    columns = [swap(v, xo) for xo, v in enumerate(sent, 1)]

    def combine(parts, refs, carried, outs):
        return call(
            functools.partial(combine_kernel, n, cap, feats, parts, bool(carried)),
            "combine",
            outs,
            [me_arr, ids_t, metas, *refs, *carried],
            scalars=1,
        )

    parts = [(0, 0, 0), (nx, 1, 0)] + [(k, i, 0) for i, k in enumerate(far + now, 2)]
    sums = combine(
        parts,
        [own, near, *early, *middle],
        [],
        [shape(feats, n * toks, dtype=F32), shape(2, 16, toks, dtype=F32)],
    )

    tile_w = 256
    out_spec = pl.BlockSpec((1, block, tile_w), lambda i: (0, 0, i))
    grad_gate_w, grad_up_w = run(
        functools.partial(weights_kernel, ndp),
        "weights",
        [shape(1, block, h)] * 2,
        [x_keep, x_came, *g_parts, g_stack],
        [whole((ny, rows, block))] * 2
        + [pl.BlockSpec((2, rows, tile_w), lambda i: (0, 0, i))] * ny
        + [pl.BlockSpec((ny, 2, rows, tile_w), lambda i: (0, 0, 0, i))],
        [out_spec, out_spec],
        grid=(h // tile_w,),
    )

    parts = [(k, i, 0) for i, k in enumerate(held)]
    for xo in range(1, nx):
        ref = len(parts) if xo == 1 else ref + 1
        parts = parts + [(xo, ref, 0), (nx + xo, ref, size)]
    summed, gg = combine(
        parts,
        [*late, *columns],
        sums,
        [shape(feats, n * toks), shape(2, toks)],
    )
    return summed.T, grad_gate_w, grad_up_w, gg.T


def solution(mesh):
    placed = (
        P(("dp", "expert"), None),
        P(("dp", "expert"), None),
        P(("dp", "expert"), None),
        P(("dp", "expert"), None),
        P("expert", None, None),
        P("expert", None, None),
        P("expert", None, None),
    )
    return jax.shard_map(
        local,
        mesh=mesh,
        in_specs=placed,
        out_specs=(
            P("dp", "expert"),
            P("expert", "dp", None),
            P("expert", "dp", None),
            P(("dp", "expert"), None),
        ),
        check_vma=False,
    )
```

```python
import functools

import jax
import jax.numpy as jnp
from jax import lax
from jax.experimental import pallas as pl
from jax.experimental.pallas import tpu as pltpu
from jax.sharding import PartitionSpec as P

F32 = jnp.float32
BF16 = jnp.bfloat16
NT = (((1,), (1,)), ((), ()))
TN = (((0,), (0,)), ((), ()))


def params(mib=48):
    return pltpu.CompilerParams(vmem_limit_bytes=mib << 20)


def vmem(count):
    return [pl.BlockSpec(memory_space=pltpu.VMEM)] * count


def smem():
    return pl.BlockSpec(memory_space=pltpu.SMEM)


LONG = 1 << 40


def pick_rows(cap, code, meta, tokens, dest):
    toks, d = tokens.shape
    slot = lax.broadcasted_iota(jnp.int32, (cap, toks), 0).astype(F32)
    for j, ref, at in dest:
        pick = (slot == code[j : j + 1, :]).astype(F32).astype(BF16)
        chosen = jnp.dot(pick, tokens, preferred_element_type=F32).astype(BF16)
        ref[at : at + cap, 0:d] = chosen
        if ref.shape[1] > d:
            add_routing(ref, at, cap, d, meta)


def add_routing(ref, at, count, d, meta):
    ref[at : at + count, d:] = jnp.zeros((count, meta.shape[1]), BF16)
    ref[at : at + meta.shape[0], d:] = meta


def prep_kernel(n, nx, cap, me_ref, *refs):
    sources, meta_ref, out_refs = refs[:4], refs[4], refs[5:-5]
    held, sems = refs[-5:-1], refs[-1]
    copies = [
        pltpu.make_async_copy(src, dst, sems.at[i])
        for i, (src, dst) in enumerate(zip(sources, held))
    ]
    for copy in copies:
        copy.start()
    ids_ref, gates_ref, tok_ref, cot_ref = held
    copies[0].wait()
    copies[1].wait()
    toks = tok_ref.shape[0]
    nz = n // nx
    expert = lax.broadcasted_iota(jnp.int32, (n, toks), 0) ^ me_ref[0]
    first = ids_ref[0:1, :] == expert
    second = ids_ref[1:2, :] == expert
    count = (first | second).astype(F32)
    before = (
        lax.broadcasted_iota(jnp.int32, (toks, toks), 0)
        < lax.broadcasted_iota(jnp.int32, (toks, toks), 1)
    ).astype(F32)
    position = jnp.dot(count.astype(BF16), before.astype(BF16), preferred_element_type=F32)
    code = jnp.where(first | second, position, -1.0)
    gates = gates_ref[...].astype(F32)
    weight = jnp.where(first, gates[0:1, :], 0.0) + jnp.where(second, gates[1:2, :], 0.0)
    meta = jnp.concatenate([code, weight], axis=0).astype(BF16)
    meta_ref[...] = meta
    near_ref, all_ref, rest, y_refs = out_refs[0], out_refs[1], out_refs[2 : 1 - nx], out_refs[1 - nx :]
    copies[2].wait()
    tokens = tok_ref[...]
    all_ref[:, 0 : tokens.shape[1]] = tokens
    add_routing(all_ref, 0, toks, tokens.shape[1], meta)
    near = [(nx + xo, near_ref, xo * cap) for xo in range(nx)]
    pick_rows(cap, code, meta, tokens, near + [(j, ref, 0) for j, ref in enumerate(rest)])
    by_column = [(zk * nx + xo, y_refs[xo - 1], zk * cap) for zk in range(nz) for xo in range(1, nx)]
    copies[3].wait()
    pick_rows(cap, code, meta, cot_ref[...], by_column)


def second_kernel(n, nx, cap, meta_ref, cot_ref, *refs):
    nz = n // nx
    came, y_refs = refs[: nx - 1], refs[nx - 1 :]
    meta = meta_ref[...]
    own = [(zk * nx, y_refs[zk], 0) for zk in range(nz)]
    pick_rows(cap, meta.astype(F32)[0:n, :], meta, cot_ref[...], own)
    for xo in range(1, nx):
        for zk in range(nz):
            y_refs[zk][xo * cap : (xo + 1) * cap, :] = came[xo - 1][zk * cap : (zk + 1) * cap, :]


def third_kernel(n, nx, cap, all_ref, near_ref, *refs):
    own, x_refs, here_ref, pass_refs = refs[: nx - 1], refs[nx - 1 : 2 * nx - 2], refs[2 * nx - 2], refs[2 * nx - 1 :]
    toks, wide = all_ref.shape
    meta = all_ref[0 : 2 * n, wide - toks :]
    dest = [(2 * nx, here_ref, 0)] + [(2 * nx + xo, x_refs[xo - 1], 2 * cap) for xo in range(1, nx)]
    dest += [(3 * nx + xo, pass_refs[xo], 0) for xo in range(nx)]
    pick_rows(cap, meta.astype(F32)[0:n, :], meta, all_ref[:, 0 : wide - toks], dest)
    for xo in range(1, nx):
        x_refs[xo - 1][0:cap, :] = own[xo - 1][...]
        x_refs[xo - 1][cap : 2 * cap, :] = near_ref[xo * cap : (xo + 1) * cap, :]


def found_x(n, nx, cap, refs):
    nz = n // nx
    z_refs, side_refs, far_refs = refs[: nz - 1], refs[nz - 1 : nz + nx - 2], refs[nz + nx - 2 :]
    found = []
    for zk in range(nz - 1):
        found += [(z_refs[zk], 0)] + [(side_refs[xo], zk * cap) for xo in range(nx - 1)]
    return found + [(ref, 0) for ref in far_refs]


def hold_kernel(in_ref, out_ref):
    out_ref[...] = in_ref[...]


def fence_kernel(out_ref):
    out_ref[...] = jnp.zeros_like(out_ref)


def forward_kernel(n, nx, cap, count, ny, place_ref, *refs):
    found = found_x(n, nx, cap, refs[:count])
    meta_ref, gate_ref, up_ref, *out_refs = refs[count:]
    part_refs, out_refs = out_refs[:ny], out_refs[ny:]
    hidden_ref, pa_ref, pb_ref, metas_ref, w_ref, rows_ref = out_refs
    toks = meta_ref.shape[1]
    d = rows_ref.shape[1]
    width = part_refs[0].shape[1]

    @pl.when(pl.program_id(0) == 0)
    def _():
        slot = lax.broadcasted_iota(jnp.int32, (cap, toks), 0).astype(F32)
        for j, (ref, at) in enumerate(found):
            row = j * cap
            rows_ref[row : row + cap, :] = ref[at : at + cap, 0:d]
            if j:
                metas_ref[j] = ref[at : at + 2 * n, d:]
            else:
                metas_ref[j] = meta_ref[...]
            meta = metas_ref[j].astype(F32)
            picked = jnp.where(slot == meta[j : j + 1, :], meta[n + j : n + j + 1, :], 0.0)
            total = jnp.sum(picked, axis=1, keepdims=True)
            w_ref[row : row + cap, :] = jnp.broadcast_to(total, (cap, w_ref.shape[1]))
        for yo, ref in enumerate(part_refs):
            at = pl.multiple_of((place_ref[0] ^ yo) * width, 128)
            ref[...] = rows_ref[:, pl.ds(at, width)]

    a = jnp.dot(rows_ref[...], gate_ref[0], preferred_element_type=F32)
    b = jnp.dot(rows_ref[...], up_ref[0], preferred_element_type=F32)
    w = w_ref[:, 0:1]
    sig = jax.nn.sigmoid(a)
    silu = a * sig
    hidden_ref[...] = (silu * b).astype(BF16)
    pa_ref[...] = w * b * sig * (1.0 + a * (1.0 - sig))
    pb_ref[...] = w * silu


def back_kernel(count, *refs):
    y_refs = refs[:count]
    hidden_ref, pa_ref, pb_ref, down_ref, grads_ref, score_ref, rows_ref, part_ref = refs[count:]
    step = pl.program_id(0)

    @pl.when(step == 0)
    def _():
        row = 0
        for ref in y_refs:
            rows_ref[row : row + ref.shape[0], :] = ref[...]
            row += ref.shape[0]
        part_ref[...] = jnp.zeros_like(part_ref)

    back = lax.dot_general(rows_ref[...], down_ref[0], NT, preferred_element_type=F32)
    grads_ref[0] = (back * pa_ref[...]).astype(BF16)
    grads_ref[1] = (back * pb_ref[...]).astype(BF16)
    prod = back * hidden_ref[...].astype(F32)
    part = part_ref[...]
    for c in range(prod.shape[1] // 128):
        part = part + prod[:, c * 128 : (c + 1) * 128]
    part_ref[...] = part

    @pl.when(step == pl.num_programs(0) - 1)
    def _():
        total = jnp.sum(jnp.transpose(part_ref[...]), axis=0, keepdims=True)
        shape = score_ref.shape
        top = lax.broadcasted_iota(jnp.int32, shape, 0) == 0
        score_ref[...] = jnp.where(top, jnp.broadcast_to(total, shape), 0.0).astype(BF16)


def rowgrad_kernel(places, dest_ref, grads_ref, score_ref, gate_ref, up_ref, *out_refs):
    del dest_ref
    size = gate_ref.shape[1]
    val = lax.dot_general(gate_ref[0], grads_ref[0], NT, preferred_element_type=F32)
    val = val + lax.dot_general(up_ref[0], grads_ref[1], NT, preferred_element_type=F32)
    val = val.astype(BF16)
    for i, (out, at) in enumerate(places):

        @pl.when(pl.program_id(0) == i)
        def _():
            out_refs[out][at : at + size, :] = val
            out_refs[out][at + size : at + size + 16, :] = score_ref[...]


def second_back_kernel(nx, size, came_ref, *refs):
    for i in range(nx - 1):
        out = refs[nx - 1 + i]
        out[0:size, :] = refs[i][...]
        out[size:, :] = came_ref[(i + 1) * size : (i + 2) * size, :]


def combine_kernel(n, cap, feats, parts, last, me_ref, ids_ref, metas_ref, *refs):
    me = me_ref[0]
    rows = n * cap
    toks = metas_ref.shape[2]
    metas = [metas_ref[j].astype(F32) for j in range(n)]
    if last:
        total_ref, part_ref, out_ref, gates_ref = refs[-4:]
        total = total_ref[...]
        gg = [part_ref[0], part_ref[1]]
    else:
        total_ref, part_ref = refs[-2:]
        total = jnp.zeros((feats, n * toks), F32)
        gg = [jnp.zeros((16, toks), F32)] * 2
    row = lax.broadcasted_iota(jnp.int32, (rows, n * toks), 0).astype(F32)
    for k, which, at in parts:
        wanted = []
        for j in range(n):
            code = metas[j][j ^ k : (j ^ k) + 1, :]
            wanted.append(jnp.where(code >= 0.0, code + float((j ^ k) * cap), -1.0))
        wanted = jnp.concatenate(wanted, axis=1)
        pick = (row == wanted).astype(F32).astype(BF16)
        got = refs[which][at : at + feats, :]
        total = total + jnp.dot(got, pick, preferred_element_type=F32)
        got = refs[which][at + feats : at + feats + 16, :]
        score = jnp.dot(got, pick[:, 0:toks], preferred_element_type=F32)
        gg = [gg[c] + jnp.where(ids_ref[c : c + 1, :] == (me ^ k), score, 0.0) for c in (0, 1)]
    if not last:
        total_ref[...] = total
        part_ref[0] = gg[0]
        part_ref[1] = gg[1]
        return
    for j in range(n):
        place = pl.multiple_of((me ^ j) * toks, toks)
        out_ref[:, pl.ds(place, toks)] = total[:, j * toks : (j + 1) * toks].astype(BF16)
    gates_ref[...] = jnp.concatenate([gg[0][0:1], gg[1][0:1]], axis=0).astype(BF16)


def first_weights_kernel(rows, core_ref, x_ref, x_came_ref, g_ref, g_came_ref, out_ref, mark_ref, xt_ref, both_ref):
    block = xt_ref.shape[0]

    @pl.when(pl.program_id(0) == 0)
    def _():
        mark_ref[...] = jnp.zeros_like(mark_ref)
        take_halves(rows, block, core_ref, x_ref, x_came_ref, xt_ref, 0)

    for half in range(2):
        both_ref[0:rows] = g_ref[half]
        both_ref[rows:] = g_came_ref[half]
        out_ref[half] = jnp.dot(xt_ref[...], both_ref[...], preferred_element_type=F32).astype(BF16)


def take_halves(rows, block, core_ref, x_ref, x_came_ref, xt_ref, at):
    @pl.when(core_ref[0] == 0)
    def _():
        xt_ref[:, at : at + rows] = x_ref[:, :block].T
        xt_ref[:, at + rows : at + 2 * rows] = x_came_ref[:, :block].T

    @pl.when(core_ref[0] != 0)
    def _():
        xt_ref[:, at : at + rows] = x_ref[:, block:].T
        xt_ref[:, at + rows : at + 2 * rows] = x_came_ref[:, block:].T


def rest_weights_kernel(rows, others, core_ref, *refs):
    x_refs, refs = refs[: 2 * others], refs[2 * others :]
    g_refs, part_ref = refs[: 2 * others], refs[2 * others]
    gate_ref, up_ref, mark_ref, xt_ref, all_ref = refs[2 * others + 1 :]
    block = xt_ref.shape[0]

    @pl.when(pl.program_id(0) == 0)
    def _():
        mark_ref[...] = jnp.zeros_like(mark_ref)
        for i in range(others):
            take_halves(rows, block, core_ref, x_refs[2 * i], x_refs[2 * i + 1], xt_ref, 2 * i * rows)

    for half, out in ((0, gate_ref), (1, up_ref)):
        for i, ref in enumerate(g_refs):
            all_ref[i * rows : (i + 1) * rows] = ref[half]
        total = jnp.dot(xt_ref[...], all_ref[...], preferred_element_type=F32)
        total = total + part_ref[half].astype(F32)
        out[0] = (total * (1.0 / (2 * others + 2))).astype(BF16)


def local(tokens, cotangent, gates, expert_ids, gate_w, up_w, down_w):
    toks, d = tokens.shape
    top = expert_ids.shape[1]
    h = gate_w.shape[2]
    n = lax.axis_size("expert")
    ndp = lax.axis_size("dp")
    nz = 4
    nx = n // nz
    ny = ndp // 2
    cap = -(-(3 * toks * top // (2 * n)) // 16) * 16
    rows = n * cap
    feats = d // n
    size = feats + 16
    block = d // ndp
    wide = d + toks
    me = lax.axis_index("expert").astype(jnp.int32)
    my_dp = lax.axis_index("dp").astype(jnp.int32)
    me_arr = me.reshape(1)
    my_y, my_core = (my_dp // 2).reshape(1), (my_dp % 2).reshape(1)
    ids_t = expert_ids.T
    gates_t = gates.T
    any_space = pl.BlockSpec(memory_space=pl.ANY)

    def swap(v, k):
        return lax.ppermute(v, "expert", [(i, i ^ k) for i in range(n)])

    def swap_dp(v, q):
        return lax.ppermute(v, "dp", [(i, i ^ q) for i in range(ndp)])

    def shape(*dims, dtype=BF16):
        return jax.ShapeDtypeStruct(dims, dtype)

    previous = []

    def run(body, name, outs, args, in_specs, out_specs, after=(), grid=(), scalars=0, scratch=(), weight=LONG, mib=48):
        waits = [*after, *previous]
        first = len(args)

        def trimmed(*refs):
            body(*refs[:first], *refs[first + len(waits) :])

        made = pl.pallas_call(
            trimmed,
            grid_spec=pltpu.PrefetchScalarGridSpec(
                num_scalar_prefetch=scalars,
                grid=grid,
                in_specs=[*in_specs, *[any_space] * len(waits)],
                out_specs=out_specs,
                scratch_shapes=scratch,
            ),
            out_shape=outs,
            compiler_params=params(mib),
            cost_estimate=pl.CostEstimate(flops=weight, bytes_accessed=1, transcendentals=0),
            name=name,
        )(*args, *waits)
        previous[:] = [min(made, key=lambda v: v.size)]
        return made

    whole = lambda dims: pl.BlockSpec(dims, lambda *_: (0,) * len(dims))

    def call(body, name, outs, args, after=(), scalars=0, **kinds):
        in_specs = [smem()] * scalars + vmem(len(args) - scalars)
        return run(body, name, outs, args, in_specs, vmem(len(outs)), after, **kinds)

    def fence(after):
        call(fence_kernel, "fence", [shape(8, 128, dtype=F32)], [], after)

    sources = [ids_t, gates_t, tokens, cotangent]
    outs = (
        [shape(2 * n, toks), shape(nx * cap, wide), shape(toks, wide), shape(cap, d)]
        + [shape(cap, wide)] * (nx - 1)
        + [shape(nz * cap, d)] * (nx - 1)
    )
    meta, x_near, x_all, x_own, *made = run(
        functools.partial(prep_kernel, n, nx, cap),
        "prep",
        outs,
        [me_arr, *sources],
        [smem()] + [pl.BlockSpec(memory_space=pltpu.HBM)] * len(sources),
        vmem(len(outs)),
        scratch=[pltpu.VMEM(v.shape, v.dtype) for v in sources]
        + [pltpu.SemaphoreType.DMA((len(sources),))],
        mib=59,
    )
    x_side, y_side = made[: nx - 1], made[nx - 1 :]
    x_near = swap(x_near, nx)
    x_all = swap(x_all, 2 * nx)
    y_side = [swap(v, xo) for xo, v in enumerate(y_side, 1)]
    y_sent = call(
        functools.partial(second_kernel, n, nx, cap),
        "second",
        [shape(nx * cap, d)] * nz,
        [meta, cotangent, *y_side],
        mib=59,
    )
    made = call(
        functools.partial(third_kernel, n, nx, cap),
        "third",
        [shape((nz - 1) * cap, wide)] * (nx - 1) + [shape(cap, wide)] * (1 + nx),
        [x_all, x_near, *x_side],
        mib=59,
    )
    x_side = [swap(v, xo) for xo, v in enumerate(made[: nx - 1], 1)]
    x_mid, x_passed = made[nx - 1], made[nx:]
    x_far = [swap(v, nx + xo) for xo, v in enumerate(x_passed)]
    y_z = [swap(y_sent[zk], zk * nx) for zk in range(2, nz)]
    got_x = [x_own, x_near, x_mid, *x_side, *x_far]
    y_near = call(hold_kernel, "hold", [shape(nx * cap, d)], [y_sent[1]], x_far, mib=59)[0]
    y_near = swap(y_near, nx)

    tile = 256
    steps = h // tile
    column = pl.BlockSpec((rows, tile), lambda i: (0, i))
    *x_parts, hidden, pa, pb, metas = run(
        functools.partial(forward_kernel, n, nx, cap, len(got_x), ny),
        "forward",
        [shape(rows, 2 * block)] * ny
        + [shape(rows, h), shape(rows, h, dtype=F32), shape(rows, h, dtype=F32)]
        + [shape(n, 2 * n, toks)],
        [my_y, *got_x, meta, gate_w, up_w],
        [smem()]
        + [whole(v.shape) for v in got_x]
        + [whole((2 * n, toks))]
        + [pl.BlockSpec((1, d, tile), lambda i: (0, 0, i))] * 2,
        [whole((rows, 2 * block))] * ny
        + [column] * 3
        + [whole((n, 2 * n, toks))],
        grid=(steps,),
        scratch=[pltpu.VMEM((rows, 128), F32), pltpu.VMEM((rows, d), BF16)],
        weight=1,
    )
    x_own_came = swap_dp(x_parts[0], 1)
    x_parts = [x_parts[0]] + [swap_dp(v, 2 * yo) for yo, v in enumerate(x_parts[1:], 1)]
    fence(y_z)
    got_y = [y_sent[0], y_near, *y_z]
    grads, score = run(
        functools.partial(back_kernel, len(got_y)),
        "back",
        [shape(2, rows, h), shape(16, rows)],
        [*got_y, hidden, pa, pb, down_w],
        [whole(v.shape) for v in got_y]
        + [column] * 3
        + [pl.BlockSpec((1, tile, d), lambda i: (0, i, 0))],
        [pl.BlockSpec((2, rows, tile), lambda i: (0, 0, i)), whole((16, rows))],
        after=[x_own_came],
        grid=(steps,),
        scratch=[pltpu.VMEM((rows, d), BF16), pltpu.VMEM((rows, 128), F32)],
        weight=1,
        mib=59,
    )
    g_own_came = swap_dp(grads, 1)
    g_parts = [grads] + [swap_dp(grads, 2 * yo) for yo in range(1, ny)]

    def rowgrads(places, outs, after=(), weight=1):
        def owner(i, me_ref):
            k = jnp.int32(places[0][0])
            for at, (other, _, _) in enumerate(places):
                k = jnp.where(i == at, other, k)
            return (0, k ^ me_ref[0], 0)

        spec = pl.BlockSpec((1, feats, h), owner)
        fixed = whole
        return run(
            functools.partial(rowgrad_kernel, [(out, at) for _, out, at in places]),
            "rowgrad",
            [shape(size * many, rows) for many in outs],
            [me_arr, grads, score, gate_w, up_w],
            [fixed((2, rows, h)), fixed((16, rows)), spec, spec],
            [fixed((size * many, rows)) for many in outs],
            after,
            grid=(len(places),),
            scalars=1,
            weight=weight,
            mib=59,
        )

    far = list(range(n - nx, n))
    mids = list(range(2 * nx, n - nx))
    straight = {}

    def send(ks, values):
        for k, v in zip(ks, values):
            straight[k] = swap(v, k)

    send(far[1:], rowgrads([(k, i, 0) for i, k in enumerate(far[1:])], [1] * (nx - 1)))
    near, sent = rowgrads(
        [(nx + xo, 0, xo * size) for xo in range(nx)] + [(far[0], 1, 0)],
        [nx, 1],
        x_parts[1:],
        weight=LONG,
    )
    near = swap(near, nx)
    send(far[:1], [sent])
    tile_w = 256
    part_spec = pl.BlockSpec((2, block, tile_w), lambda i: (0, 0, i))
    column_w = pl.BlockSpec((2, rows, tile_w), lambda i: (0, 0, i))
    x_spec = whole((rows, 2 * block))
    w_part, _ = run(
        functools.partial(first_weights_kernel, rows),
        "weights",
        [shape(2, block, h), shape(8, 128, dtype=F32)],
        [my_core, x_parts[0], x_own_came, grads, g_own_came],
        [smem(), x_spec, x_spec, column_w, column_w],
        [part_spec, whole((8, 128))],
        grid=(h // tile_w,),
        scratch=[pltpu.VMEM((block, 2 * rows), BF16), pltpu.VMEM((2 * rows, tile_w), BF16)],
    )
    x_came = [swap_dp(v, 1) for v in x_parts[1:]]
    last = mids[::-1]
    own, *sent = rowgrads(
        [(k, i, 0) for i, k in enumerate([0, *range(1, nx), *last])],
        [1] * (nx + len(last)),
        x_came,
        weight=LONG,
    )
    by_column, sent = sent[: nx - 1], sent[nx - 1 :]
    send(last, sent)

    g_came = [swap_dp(v, 1) for v in g_parts[1:]]
    fence(g_parts[1:])

    sent = call(
        functools.partial(second_back_kernel, nx, size),
        "second_back",
        [shape(2 * size, rows)] * (nx - 1),
        [near, *by_column],
        [straight[k] for k in far[1:]],
    )
    columns = [swap(v, xo) for xo, v in enumerate(sent, 1)]

    def combine(parts, refs, carried, outs):
        return call(
            functools.partial(combine_kernel, n, cap, feats, parts, bool(carried)),
            "combine",
            outs,
            [me_arr, ids_t, metas, *refs, *carried],
            scalars=1,
        )

    parts = [(0, 0, 0), (nx, 1, 0)] + [(k, i, 0) for i, k in enumerate(far, 2)]
    sums = combine(
        parts,
        [own, near, *[straight[k] for k in far]],
        [],
        [shape(feats, n * toks, dtype=F32), shape(2, 16, toks, dtype=F32)],
    )

    others = ny - 1
    out_spec = pl.BlockSpec((1, block, tile_w), lambda i: (0, 0, i))
    pairs = lambda ours, theirs: [v for both in zip(ours, theirs) for v in both]
    grad_gate_w, grad_up_w, _ = run(
        functools.partial(rest_weights_kernel, rows, others),
        "weights_rest",
        [shape(1, block, h)] * 2 + [shape(8, 128, dtype=F32)],
        [my_core, *pairs(x_parts[1:], x_came), *pairs(g_parts[1:], g_came), w_part],
        [smem()] + [x_spec] * (2 * others) + [column_w] * (2 * others) + [part_spec],
        [out_spec, out_spec, whole((8, 128))],
        grid=(h // tile_w,),
        scratch=[
            pltpu.VMEM((block, 2 * others * rows), BF16),
            pltpu.VMEM((2 * others * rows, tile_w), BF16),
        ],
    )

    parts = [(k, i, 0) for i, k in enumerate(last)]
    for i in range(nx - 1):
        parts += [(i + 1, len(last) + i, 0), (nx + i + 1, len(last) + i, size)]
    summed, gg = combine(
        parts,
        [*[straight[k] for k in last], *columns],
        sums,
        [shape(feats, n * toks), shape(2, toks)],
    )
    return summed.T, grad_gate_w, grad_up_w, gg.T


def solution(mesh):
    placed = (
        P(("dp", "expert"), None),
        P(("dp", "expert"), None),
        P(("dp", "expert"), None),
        P(("dp", "expert"), None),
        P("expert", None, None),
        P("expert", None, None),
        P("expert", None, None),
    )
    return jax.shard_map(
        local,
        mesh=mesh,
        in_specs=placed,
        out_specs=(
            P("dp", "expert"),
            P("expert", "dp", None),
            P("expert", "dp", None),
            P(("dp", "expert"), None),
        ),
        check_vma=False,
    )
```

```python
import functools

import jax
import jax.numpy as jnp
from jax import lax
from jax.experimental import pallas as pl
from jax.experimental.pallas import tpu as pltpu
from jax.sharding import PartitionSpec as P

F32 = jnp.float32
BF16 = jnp.bfloat16
NT = (((1,), (1,)), ((), ()))
TN = (((0,), (0,)), ((), ()))


def params(mib=48):
    return pltpu.CompilerParams(vmem_limit_bytes=mib << 20)


def vmem(count):
    return [pl.BlockSpec(memory_space=pltpu.VMEM)] * count


def smem():
    return pl.BlockSpec(memory_space=pltpu.SMEM)


LONG = 1 << 40


def pick_rows(cap, code, meta, tokens, dest):
    toks, d = tokens.shape
    slot = lax.broadcasted_iota(jnp.int32, (cap, toks), 0).astype(F32)
    for j, ref, at in dest:
        pick = (slot == code[j : j + 1, :]).astype(F32).astype(BF16)
        chosen = jnp.dot(pick, tokens, preferred_element_type=F32).astype(BF16)
        ref[at : at + cap, 0:d] = chosen
        if ref.shape[1] > d:
            add_routing(ref, at, cap, d, meta)


def add_routing(ref, at, count, d, meta):
    ref[at : at + count, d:] = jnp.zeros((count, meta.shape[1]), BF16)
    ref[at : at + meta.shape[0], d:] = meta


def prep_kernel(n, nx, cap, me_ref, *refs):
    sources, meta_ref, out_refs = refs[:4], refs[4], refs[5:-5]
    held, sems = refs[-5:-1], refs[-1]
    copies = [
        pltpu.make_async_copy(src, dst, sems.at[i])
        for i, (src, dst) in enumerate(zip(sources, held))
    ]
    for copy in copies:
        copy.start()
    ids_ref, gates_ref, tok_ref, cot_ref = held
    copies[0].wait()
    copies[1].wait()
    toks = tok_ref.shape[0]
    nz = n // nx
    expert = lax.broadcasted_iota(jnp.int32, (n, toks), 0) ^ me_ref[0]
    first = ids_ref[0:1, :] == expert
    second = ids_ref[1:2, :] == expert
    count = (first | second).astype(F32)
    before = (
        lax.broadcasted_iota(jnp.int32, (toks, toks), 0)
        < lax.broadcasted_iota(jnp.int32, (toks, toks), 1)
    ).astype(F32)
    position = jnp.dot(count.astype(BF16), before.astype(BF16), preferred_element_type=F32)
    code = jnp.where(first | second, position, -1.0)
    gates = gates_ref[...].astype(F32)
    weight = jnp.where(first, gates[0:1, :], 0.0) + jnp.where(second, gates[1:2, :], 0.0)
    meta = jnp.concatenate([code, weight], axis=0).astype(BF16)
    meta_ref[...] = meta
    halves = 2 * (nx - 1)
    near_ref, rest, y_refs = out_refs[0], out_refs[1:-halves], out_refs[-halves:]
    copies[2].wait()
    tokens = tok_ref[...]
    near = [(nx + xo, near_ref, xo * cap) for xo in range(nx)]
    pick_rows(cap, code, meta, tokens, near + [(j, ref, 0) for j, ref in enumerate(rest)])
    by_column = [
        (zk * nx + xo, y_refs[2 * xo - 2 + zk // 2], zk % 2 * cap) for zk in range(nz) for xo in range(1, nx)
    ]
    copies[3].wait()
    pick_rows(cap, code, meta, cot_ref[...], by_column)


def second_kernel(n, nx, cap, meta_ref, cot_ref, *refs):
    nz = n // nx
    came, y_refs = refs[: 2 * nx - 2], refs[2 * nx - 2 :]
    meta = meta_ref[...]
    own = [(zk * nx, y_refs[zk], 0) for zk in range(nz)]
    pick_rows(cap, meta.astype(F32)[0:n, :], meta, cot_ref[...], own)
    for xo in range(1, nx):
        for zk in range(nz):
            at = zk % 2 * cap
            y_refs[zk][xo * cap : (xo + 1) * cap, :] = came[2 * xo - 2 + zk // 2][at : at + cap, :]


def third_kernel(n, nx, cap, all_ref, meta_ref, near_ref, *refs):
    own, x_refs, here_ref, pass_refs = refs[: nx - 1], refs[nx - 1 : 2 * nx - 2], refs[2 * nx - 2], refs[2 * nx - 1 :]
    meta = meta_ref[...]
    dest = [(2 * nx, here_ref, 0)] + [(2 * nx + xo, x_refs[xo - 1], 2 * cap) for xo in range(1, nx)]
    dest += [(3 * nx + xo, pass_refs[xo], 0) for xo in range(nx)]
    pick_rows(cap, meta.astype(F32)[0:n, :], meta, all_ref[...], dest)
    for xo in range(1, nx):
        x_refs[xo - 1][0:cap, :] = own[xo - 1][...]
        x_refs[xo - 1][cap : 2 * cap, :] = near_ref[xo * cap : (xo + 1) * cap, :]


def found_x(n, nx, cap, refs):
    nz = n // nx
    z_refs, side_refs, far_refs = refs[: nz - 1], refs[nz - 1 : nz + nx - 2], refs[nz + nx - 2 :]
    found = []
    for zk in range(nz - 1):
        found += [(z_refs[zk], 0)] + [(side_refs[xo], zk * cap) for xo in range(nx - 1)]
    return found + [(ref, 0) for ref in far_refs]


def hold_kernel(in_ref, out_ref):
    out_ref[...] = in_ref[...]


def copy_kernel(*refs):
    count = len(refs) // 2
    for src, out in zip(refs[:count], refs[count:]):
        out[...] = src[...]


def fence_kernel(out_ref):
    out_ref[...] = jnp.zeros_like(out_ref)


def gather_kernel(n, nx, cap, count, ny, place_ref, *refs):
    found = found_x(n, nx, cap, refs[:count])
    meta_ref, *part_refs = refs[count : count + 1 + ny]
    rows_ref, w_ref, metas_ref = refs[count + 1 + ny :]
    toks = meta_ref.shape[1]
    d = rows_ref.shape[1]
    slot = lax.broadcasted_iota(jnp.int32, (cap, toks), 0).astype(F32)
    for j, (ref, at) in enumerate(found):
        row = j * cap
        rows_ref[row : row + cap, :] = ref[at : at + cap, 0:d]
        if j:
            metas_ref[j] = ref[at : at + 2 * n, d:]
        else:
            metas_ref[j] = meta_ref[...]
        meta = metas_ref[j].astype(F32)
        picked = jnp.where(slot == meta[j : j + 1, :], meta[n + j : n + j + 1, :], 0.0)
        total = jnp.sum(picked, axis=1, keepdims=True)
        w_ref[row : row + cap, :] = jnp.broadcast_to(total, (cap, w_ref.shape[1]))
    width = part_refs[0].shape[1]
    for yo, ref in enumerate(part_refs):
        at = pl.multiple_of((place_ref[0] ^ yo) * width, 128)
        ref[...] = rows_ref[:, pl.ds(at, width)]


def forward_kernel(rows_ref, w_ref, gate_ref, up_ref, hidden_ref, pa_ref, pb_ref):
    a = jnp.dot(rows_ref[...], gate_ref[0], preferred_element_type=F32)
    b = jnp.dot(rows_ref[...], up_ref[0], preferred_element_type=F32)
    w = w_ref[:, 0:1]
    sig = jax.nn.sigmoid(a)
    silu = a * sig
    hidden_ref[...] = (silu * b).astype(BF16)
    pa_ref[...] = w * b * sig * (1.0 + a * (1.0 - sig))
    pb_ref[...] = w * silu


def back_kernel(count, steps, me_ref, *refs):
    del me_ref
    y_refs = refs[:count]
    hidden_ref, pa_ref, pb_ref, down_ref, gate_ref, up_ref, grads_ref, score_ref, *refs = refs[count:]
    out_refs, (rows_ref, part_ref, all_ref) = refs[:-3], refs[-3:]
    step = pl.program_id(0)
    tile = down_ref.shape[1]
    feats = gate_ref.shape[1]

    @pl.when(step == 0)
    def _():
        row = 0
        for ref in y_refs:
            rows_ref[row : row + ref.shape[0], :] = ref[...]
            row += ref.shape[0]
        part_ref[...] = jnp.zeros_like(part_ref)

    @pl.when(step < steps)
    def _():
        back = lax.dot_general(rows_ref[...], down_ref[0], NT, preferred_element_type=F32)
        da = (back * pa_ref[...]).astype(BF16)
        db = (back * pb_ref[...]).astype(BF16)
        grads_ref[0] = da
        grads_ref[1] = db
        at = pl.ds(pl.multiple_of(step * tile, tile), tile)
        all_ref[0, :, at] = da
        all_ref[1, :, at] = db
        prod = back * hidden_ref[...].astype(F32)
        part = part_ref[...]
        for c in range(prod.shape[1] // 128):
            part = part + prod[:, c * 128 : (c + 1) * 128]
        part_ref[...] = part

    @pl.when(step == steps - 1)
    def _():
        total = jnp.sum(jnp.transpose(part_ref[...]), axis=0, keepdims=True)
        shape = score_ref.shape
        top = lax.broadcasted_iota(jnp.int32, shape, 0) == 0
        score_ref[...] = jnp.where(top, jnp.broadcast_to(total, shape), 0.0).astype(BF16)

    @pl.when(step >= steps)
    def _():
        val = lax.dot_general(gate_ref[0], all_ref[0], NT, preferred_element_type=F32)
        val = val + lax.dot_general(up_ref[0], all_ref[1], NT, preferred_element_type=F32)
        val = val.astype(BF16)
        for i, out in enumerate(out_refs):

            @pl.when(step == steps + i)
            def _():
                out[0:feats, :] = val
                out[feats:, :] = score_ref[...]


def rowgrad_kernel(places, dest_ref, grads_ref, score_ref, gate_ref, up_ref, *out_refs):
    del dest_ref
    size = gate_ref.shape[1]
    val = lax.dot_general(gate_ref[0], grads_ref[0], NT, preferred_element_type=F32)
    val = val + lax.dot_general(up_ref[0], grads_ref[1], NT, preferred_element_type=F32)
    val = val.astype(BF16)
    for i, (out, at) in enumerate(places):

        @pl.when(pl.program_id(0) == i)
        def _():
            out_refs[out][at : at + size, :] = val
            out_refs[out][at + size : at + size + 16, :] = score_ref[...]


def second_back_kernel(nx, size, came_ref, *refs):
    for i in range(nx - 1):
        out = refs[nx - 1 + i]
        out[0:size, :] = refs[i][...]
        out[size:, :] = came_ref[(i + 1) * size : (i + 2) * size, :]


def combine_kernel(n, cap, feats, parts, more, last, me_ref, ids_ref, metas_ref, *refs):
    me = me_ref[0]
    rows = n * cap
    toks = metas_ref.shape[2]
    metas = [metas_ref[j].astype(F32) for j in range(n)]
    if more:
        total = refs[-4][...]
        gg = [refs[-3][0], refs[-3][1]]
    else:
        total = jnp.zeros((feats, n * toks), F32)
        gg = [jnp.zeros((16, toks), F32)] * 2
    out_ref, gates_ref = refs[-2:]
    row = lax.broadcasted_iota(jnp.int32, (rows, n * toks), 0).astype(F32)
    for k, which, at in parts:
        wanted = []
        for j in range(n):
            code = metas[j][j ^ k : (j ^ k) + 1, :]
            wanted.append(jnp.where(code >= 0.0, code + float((j ^ k) * cap), -1.0))
        wanted = jnp.concatenate(wanted, axis=1)
        pick = (row == wanted).astype(F32).astype(BF16)
        got = refs[which][at : at + feats, :]
        total = total + jnp.dot(got, pick, preferred_element_type=F32)
        got = refs[which][at + feats : at + feats + 16, :]
        score = jnp.dot(got, pick[:, 0:toks], preferred_element_type=F32)
        gg = [gg[c] + jnp.where(ids_ref[c : c + 1, :] == (me ^ k), score, 0.0) for c in (0, 1)]
    if not last:
        out_ref[...] = total
        gates_ref[0] = gg[0]
        gates_ref[1] = gg[1]
        return
    for j in range(n):
        place = pl.multiple_of((me ^ j) * toks, toks)
        out_ref[:, pl.ds(place, toks)] = total[:, j * toks : (j + 1) * toks].astype(BF16)
    gates_ref[...] = jnp.concatenate([gg[0][0:1], gg[1][0:1]], axis=0).astype(BF16)


def first_weights_kernel(rows, core_ref, x_ref, x_came_ref, g_ref, g_came_ref, out_ref, mark_ref, xt_ref, both_ref):
    block = xt_ref.shape[0]

    @pl.when(pl.program_id(0) == 0)
    def _():
        mark_ref[...] = jnp.zeros_like(mark_ref)
        take_halves(rows, block, core_ref, x_ref, x_came_ref, xt_ref, 0)

    for half in range(2):
        both_ref[0:rows] = g_ref[half]
        both_ref[rows:] = g_came_ref[half]
        out_ref[half] = jnp.dot(xt_ref[...], both_ref[...], preferred_element_type=F32).astype(BF16)


def take_halves(rows, block, core_ref, x_ref, x_came_ref, xt_ref, at):
    @pl.when(core_ref[0] == 0)
    def _():
        xt_ref[:, at : at + rows] = x_ref[:, :block].T
        xt_ref[:, at + rows : at + 2 * rows] = x_came_ref[:, :block].T

    @pl.when(core_ref[0] != 0)
    def _():
        xt_ref[:, at : at + rows] = x_ref[:, block:].T
        xt_ref[:, at + rows : at + 2 * rows] = x_came_ref[:, block:].T


def rest_weights_kernel(rows, others, core_ref, *refs):
    x_refs, refs = refs[: 2 * others], refs[2 * others :]
    g_refs, part_ref = refs[: 2 * others], refs[2 * others]
    gate_ref, up_ref, mark_ref, xt_ref, all_ref = refs[2 * others + 1 :]
    block = xt_ref.shape[0]

    @pl.when(pl.program_id(0) == 0)
    def _():
        mark_ref[...] = jnp.zeros_like(mark_ref)
        for i in range(others):
            take_halves(rows, block, core_ref, x_refs[2 * i], x_refs[2 * i + 1], xt_ref, 2 * i * rows)

    for half, out in ((0, gate_ref), (1, up_ref)):
        for i, ref in enumerate(g_refs):
            all_ref[i * rows : (i + 1) * rows] = ref[half]
        total = jnp.dot(xt_ref[...], all_ref[...], preferred_element_type=F32)
        total = total + part_ref[half].astype(F32)
        out[0] = (total * (1.0 / (2 * others + 2))).astype(BF16)


def local(tokens, cotangent, gates, expert_ids, gate_w, up_w, down_w):
    toks, d = tokens.shape
    top = expert_ids.shape[1]
    h = gate_w.shape[2]
    n = lax.axis_size("expert")
    ndp = lax.axis_size("dp")
    nz = 4
    nx = n // nz
    ny = ndp // 2
    cap = -(-(3 * toks * top // (2 * n)) // 16) * 16
    rows = n * cap
    feats = d // n
    size = feats + 16
    block = d // ndp
    wide = d + toks
    me = lax.axis_index("expert").astype(jnp.int32)
    my_dp = lax.axis_index("dp").astype(jnp.int32)
    me_arr = me.reshape(1)
    my_y, my_core = (my_dp // 2).reshape(1), (my_dp % 2).reshape(1)
    ids_t = expert_ids.T
    gates_t = gates.T
    any_space = pl.BlockSpec(memory_space=pl.ANY)

    def swap(v, k):
        return lax.ppermute(v, "expert", [(i, i ^ k) for i in range(n)])

    def swap_dp(v, q):
        return lax.ppermute(v, "dp", [(i, i ^ q) for i in range(ndp)])

    def shape(*dims, dtype=BF16):
        return jax.ShapeDtypeStruct(dims, dtype)

    previous = []

    def run(body, name, outs, args, in_specs, out_specs, after=(), grid=(), scalars=0, scratch=(), weight=LONG, mib=48):
        waits = [*after, *previous]
        first = len(args)

        def trimmed(*refs):
            body(*refs[:first], *refs[first + len(waits) :])

        made = pl.pallas_call(
            trimmed,
            grid_spec=pltpu.PrefetchScalarGridSpec(
                num_scalar_prefetch=scalars,
                grid=grid,
                in_specs=[*in_specs, *[any_space] * len(waits)],
                out_specs=out_specs,
                scratch_shapes=scratch,
            ),
            out_shape=outs,
            compiler_params=params(mib),
            cost_estimate=pl.CostEstimate(flops=weight, bytes_accessed=1, transcendentals=0),
            name=name,
        )(*args, *waits)
        previous[:] = [min(made, key=lambda v: v.size)]
        return made

    whole = lambda dims: pl.BlockSpec(dims, lambda *_: (0,) * len(dims))

    def call(body, name, outs, args, after=(), scalars=0, **kinds):
        in_specs = [smem()] * scalars + vmem(len(args) - scalars)
        return run(body, name, outs, args, in_specs, vmem(len(outs)), after, **kinds)

    def fence(after):
        call(fence_kernel, "fence", [shape(8, 128, dtype=F32)], [], after)

    sources = [ids_t, gates_t, tokens, cotangent]
    outs = (
        [shape(2 * n, toks), shape(nx * cap, wide), shape(cap, d)]
        + [shape(cap, wide)] * (nx - 1)
        + [shape(nz // 2 * cap, d)] * (2 * nx - 2)
    )
    x_all = swap(tokens, 2 * nx)
    meta, x_near, x_own, *made = run(
        functools.partial(prep_kernel, n, nx, cap),
        "prep",
        outs,
        [me_arr, *sources],
        [smem()] + [pl.BlockSpec(memory_space=pltpu.HBM)] * len(sources),
        vmem(len(outs)),
        scratch=[pltpu.VMEM(v.shape, v.dtype) for v in sources]
        + [pltpu.SemaphoreType.DMA((len(sources),))],
        mib=59,
    )
    x_side, y_side = made[: nx - 1], made[nx - 1 :]
    x_near = swap(x_near, nx)
    meta_all = swap(meta, 2 * nx)
    y_side = [swap(v, i // 2 + 1) for i, v in enumerate(y_side)]
    y_sent = call(
        functools.partial(second_kernel, n, nx, cap),
        "second",
        [shape(nx * cap, d)] * nz,
        [meta, cotangent, *y_side],
        weight=1,
        mib=59,
    )
    made = call(
        functools.partial(third_kernel, n, nx, cap),
        "third",
        [shape((nz - 1) * cap, wide)] * (nx - 1) + [shape(cap, wide)] * (1 + nx),
        [x_all, meta_all, x_near, *x_side],
        mib=59,
        weight=1,
    )
    x_side = [swap(v, xo) for xo, v in enumerate(made[: nx - 1], 1)]
    x_mid, x_passed = made[nx - 1], made[nx:]
    x_far = [swap(v, nx + xo) for xo, v in enumerate(x_passed)]
    y_z = [swap(y_sent[zk], zk * nx) for zk in range(2, nz)]
    got_x = [x_own, x_near, x_mid, *x_side, *x_far]
    y_near = call(hold_kernel, "hold", [shape(nx * cap, d)], [y_sent[1]], x_far, mib=59)[0]
    y_near = swap(y_near, nx)

    tile = 256
    steps = h // tile
    column = pl.BlockSpec((rows, tile), lambda i: (0, i))
    *x_parts, x_rows, row_w, metas = call(
        functools.partial(gather_kernel, n, nx, cap, len(got_x), ny),
        "gather",
        [shape(rows, 2 * block)] * ny
        + [shape(rows, d), shape(rows, 128, dtype=F32), shape(n, 2 * n, toks)],
        [my_y, *got_x, meta],
        scalars=1,
        weight=1,
    )
    x_own_came = swap_dp(x_parts[0], 1)
    x_parts = [x_parts[0]] + [swap_dp(v, 2 * yo) for yo, v in enumerate(x_parts[1:], 1)]
    hidden, pa, pb = run(
        forward_kernel,
        "forward",
        [shape(rows, h), shape(rows, h, dtype=F32), shape(rows, h, dtype=F32)],
        [x_rows, row_w, gate_w, up_w],
        [whole((rows, d)), whole((rows, 128))]
        + [pl.BlockSpec((1, d, tile), lambda i: (0, 0, i))] * 2,
        [column] * 3,
        grid=(steps,),
        weight=1,
    )
    fence(y_z)
    got_y = [y_sent[0], y_near, *y_z]
    first_sent = list(range(n - nx + 1, n))
    held = lambda i: jnp.minimum(i, steps - 1)
    column_b = pl.BlockSpec((rows, tile), lambda i, _: (0, held(i)))

    def first_owner(i, me_ref):
        k = jnp.maximum(i - steps, 0) + first_sent[0]
        return (0, k ^ me_ref[0], 0)

    out_spec = pl.BlockSpec((1, feats, h), first_owner)
    grads, score, *sent = run(
        functools.partial(back_kernel, len(got_y), steps),
        "back",
        [shape(2, rows, h), shape(16, rows)] + [shape(size, rows)] * (nx - 1),
        [me_arr, *got_y, hidden, pa, pb, down_w, gate_w, up_w],
        [whole(v.shape) for v in got_y]
        + [column_b] * 3
        + [pl.BlockSpec((1, tile, d), lambda i, _: (0, held(i), 0)), out_spec, out_spec],
        [pl.BlockSpec((2, rows, tile), lambda i, _: (0, 0, held(i)))]
        + [whole((16, rows))]
        + [whole((size, rows))] * (nx - 1),
        after=[x_own_came],
        grid=(steps + nx - 1,),
        scalars=1,
        scratch=[
            pltpu.VMEM((rows, d), BF16),
            pltpu.VMEM((rows, 128), F32),
            pltpu.VMEM((2, rows, h), BF16),
        ],
        weight=1,
        mib=59,
    )
    g_own_came = swap_dp(grads, 1)
    g_parts = [grads] + [swap_dp(grads, 2 * yo) for yo in range(1, ny)]

    def rowgrads(places, outs, after=(), weight=1):
        def owner(i, me_ref):
            k = jnp.int32(places[0][0])
            for at, (other, _, _) in enumerate(places):
                k = jnp.where(i == at, other, k)
            return (0, k ^ me_ref[0], 0)

        spec = pl.BlockSpec((1, feats, h), owner)
        fixed = whole
        return run(
            functools.partial(rowgrad_kernel, [(out, at) for _, out, at in places]),
            "rowgrad",
            [shape(size * many, rows) for many in outs],
            [me_arr, grads, score, gate_w, up_w],
            [fixed((2, rows, h)), fixed((16, rows)), spec, spec],
            [fixed((size * many, rows)) for many in outs],
            after,
            grid=(len(places),),
            scalars=1,
            weight=weight,
            mib=59,
        )

    far = list(range(n - nx, n))
    mids = list(range(2 * nx, n - nx))
    straight = {}

    def send(ks, values):
        for k, v in zip(ks, values):
            straight[k] = swap(v, k)

    sent = call(
        copy_kernel, "hold", [shape(size, rows)] * (nx - 1), sent, weight=1, mib=59
    )
    send(first_sent, sent)
    near, sent = rowgrads(
        [(nx + xo, 0, xo * size) for xo in range(nx)] + [(far[0], 1, 0)],
        [nx, 1],
        x_parts[1:],
        weight=LONG,
    )
    near = swap(near, nx)
    send(far[:1], [sent])
    tile_w = 256
    part_spec = pl.BlockSpec((2, block, tile_w), lambda i: (0, 0, i))
    column_w = pl.BlockSpec((2, rows, tile_w), lambda i: (0, 0, i))
    x_spec = whole((rows, 2 * block))
    w_part, _ = run(
        functools.partial(first_weights_kernel, rows),
        "weights",
        [shape(2, block, h), shape(8, 128, dtype=F32)],
        [my_core, x_parts[0], x_own_came, grads, g_own_came],
        [smem(), x_spec, x_spec, column_w, column_w],
        [part_spec, whole((8, 128))],
        grid=(h // tile_w,),
        scratch=[pltpu.VMEM((block, 2 * rows), BF16), pltpu.VMEM((2 * rows, tile_w), BF16)],
    )
    x_came = [swap_dp(v, 1) for v in x_parts[1:]]
    last = mids[::-1]
    own, *sent = rowgrads(
        [(k, i, 0) for i, k in enumerate([0, *range(1, nx), *last])],
        [1] * (nx + len(last)),
        x_came,
        weight=LONG,
    )
    by_column, sent = sent[: nx - 1], sent[nx - 1 :]
    send(last, sent)

    g_came = [swap_dp(v, 1) for v in g_parts[1:]]
    fence(g_parts[1:])

    sent = call(
        functools.partial(second_back_kernel, nx, size),
        "second_back",
        [shape(2 * size, rows)] * (nx - 1),
        [near, *by_column],
        [straight[k] for k in far[1:]],
    )
    columns = [swap(v, xo) for xo, v in enumerate(sent, 1)]

    sum_shapes = [shape(feats, n * toks, dtype=F32), shape(2, 16, toks, dtype=F32)]

    def combine(parts, refs, carried, outs, final):
        return call(
            functools.partial(combine_kernel, n, cap, feats, parts, bool(carried), final),
            "combine",
            outs,
            [me_arr, ids_t, metas, *refs, *carried],
            scalars=1,
        )

    parts = [(0, 0, 0), (nx, 1, 0)] + [(k, i, 0) for i, k in enumerate(far, 2)]
    sums = combine(
        parts,
        [own, near, *[straight[k] for k in far]],
        [],
        sum_shapes,
        False,
    )

    others = ny - 1
    out_spec = pl.BlockSpec((1, block, tile_w), lambda i: (0, 0, i))
    pairs = lambda ours, theirs: [v for both in zip(ours, theirs) for v in both]
    grad_gate_w, grad_up_w, _ = run(
        functools.partial(rest_weights_kernel, rows, others),
        "weights_rest",
        [shape(1, block, h)] * 2 + [shape(8, 128, dtype=F32)],
        [my_core, *pairs(x_parts[1:], x_came), *pairs(g_parts[1:], g_came), w_part],
        [smem()] + [x_spec] * (2 * others) + [column_w] * (2 * others) + [part_spec],
        [out_spec, out_spec, whole((8, 128))],
        grid=(h // tile_w,),
        scratch=[
            pltpu.VMEM((block, 2 * others * rows), BF16),
            pltpu.VMEM((2 * others * rows, tile_w), BF16),
        ],
    )

    parts = []
    for i in range(nx - 1):
        parts += [(i + 1, i, 0), (nx + i + 1, i, size)]
    sums = combine(parts, columns, sums, sum_shapes, False)
    summed, gg = combine(
        [(k, i, 0) for i, k in enumerate(last)],
        [straight[k] for k in last],
        sums,
        [shape(feats, n * toks), shape(2, toks)],
        True,
    )
    return summed.T, grad_gate_w, grad_up_w, gg.T


def solution(mesh):
    placed = (
        P(("dp", "expert"), None),
        P(("dp", "expert"), None),
        P(("dp", "expert"), None),
        P(("dp", "expert"), None),
        P("expert", None, None),
        P("expert", None, None),
        P("expert", None, None),
    )
    return jax.shard_map(
        local,
        mesh=mesh,
        in_specs=placed,
        out_specs=(
            P("dp", "expert"),
            P("expert", "dp", None),
            P("expert", "dp", None),
            P(("dp", "expert"), None),
        ),
        check_vma=False,
    )
```

```python
import functools

import jax
import jax.numpy as jnp
from jax import lax
from jax.experimental import pallas as pl
from jax.experimental.pallas import tpu as pltpu
from jax.sharding import PartitionSpec as P

F32 = jnp.float32
BF16 = jnp.bfloat16
NT = (((1,), (1,)), ((), ()))
TN = (((0,), (0,)), ((), ()))


def params(mib=48):
    return pltpu.CompilerParams(vmem_limit_bytes=mib << 20)


def vmem(count):
    return [pl.BlockSpec(memory_space=pltpu.VMEM)] * count


def smem():
    return pl.BlockSpec(memory_space=pltpu.SMEM)


LONG = 1 << 40


def pick_rows(cap, code, meta, tokens, dest):
    toks, d = tokens.shape
    slot = lax.broadcasted_iota(jnp.int32, (cap, toks), 0).astype(F32)
    for j, ref, at in dest:
        pick = (slot == code[j : j + 1, :]).astype(F32).astype(BF16)
        chosen = jnp.dot(pick, tokens, preferred_element_type=F32).astype(BF16)
        ref[at : at + cap, 0:d] = chosen
        if ref.shape[1] > d:
            add_routing(ref, at, cap, d, meta)


def add_routing(ref, at, count, d, meta):
    ref[at : at + count, d:] = jnp.zeros((count, meta.shape[1]), BF16)
    ref[at : at + meta.shape[0], d:] = meta


def prep_kernel(n, nx, cap, me_ref, *refs):
    sources, meta_ref, out_refs = refs[:4], refs[4], refs[5:-5]
    held, sems = refs[-5:-1], refs[-1]
    copies = [
        pltpu.make_async_copy(src, dst, sems.at[i])
        for i, (src, dst) in enumerate(zip(sources, held))
    ]
    for copy in copies:
        copy.start()
    ids_ref, gates_ref, tok_ref, cot_ref = held
    copies[0].wait()
    copies[1].wait()
    toks = tok_ref.shape[0]
    nz = n // nx
    expert = lax.broadcasted_iota(jnp.int32, (n, toks), 0) ^ me_ref[0]
    first = ids_ref[0:1, :] == expert
    second = ids_ref[1:2, :] == expert
    count = (first | second).astype(F32)
    before = (
        lax.broadcasted_iota(jnp.int32, (toks, toks), 0)
        < lax.broadcasted_iota(jnp.int32, (toks, toks), 1)
    ).astype(F32)
    position = jnp.dot(count.astype(BF16), before.astype(BF16), preferred_element_type=F32)
    code = jnp.where(first | second, position, -1.0)
    gates = gates_ref[...].astype(F32)
    weight = jnp.where(first, gates[0:1, :], 0.0) + jnp.where(second, gates[1:2, :], 0.0)
    meta = jnp.concatenate([code, weight], axis=0).astype(BF16)
    meta_ref[...] = meta
    halves = 2 * (nx - 1)
    near_ref, rest, y_refs = out_refs[0], out_refs[1:-halves], out_refs[-halves:]
    copies[2].wait()
    tokens = tok_ref[...]
    near = [(nx + xo, near_ref, xo * cap) for xo in range(nx)]
    pick_rows(cap, code, meta, tokens, near + [(j, ref, 0) for j, ref in enumerate(rest)])
    by_column = [
        (zk * nx + xo, y_refs[2 * xo - 2 + zk // 2], zk % 2 * cap) for zk in range(nz) for xo in range(1, nx)
    ]
    copies[3].wait()
    pick_rows(cap, code, meta, cot_ref[...], by_column)


def second_kernel(n, nx, cap, meta_ref, cot_ref, *refs):
    nz = n // nx
    came, y_refs = refs[: 2 * nx - 2], refs[2 * nx - 2 :]
    meta = meta_ref[...]
    own = [(zk * nx, y_refs[zk], 0) for zk in range(nz)]
    pick_rows(cap, meta.astype(F32)[0:n, :], meta, cot_ref[...], own)
    for xo in range(1, nx):
        for zk in range(nz):
            at = zk % 2 * cap
            y_refs[zk][xo * cap : (xo + 1) * cap, :] = came[2 * xo - 2 + zk // 2][at : at + cap, :]


def third_kernel(n, nx, cap, all_ref, meta_ref, near_ref, *refs):
    own, x_refs, here_ref, pass_refs = refs[: nx - 1], refs[nx - 1 : 2 * nx - 2], refs[2 * nx - 2], refs[2 * nx - 1 :]
    meta = meta_ref[...]
    dest = [(2 * nx, here_ref, 0)] + [(2 * nx + xo, x_refs[xo - 1], 2 * cap) for xo in range(1, nx)]
    dest += [(3 * nx + xo, pass_refs[xo], 0) for xo in range(nx)]
    pick_rows(cap, meta.astype(F32)[0:n, :], meta, all_ref[...], dest)
    for xo in range(1, nx):
        x_refs[xo - 1][0:cap, :] = own[xo - 1][...]
        x_refs[xo - 1][cap : 2 * cap, :] = near_ref[xo * cap : (xo + 1) * cap, :]


def found_x(n, nx, cap, refs):
    nz = n // nx
    z_refs, side_refs, far_refs = refs[: nz - 1], refs[nz - 1 : nz + nx - 2], refs[nz + nx - 2 :]
    found = []
    for zk in range(nz - 1):
        found += [(z_refs[zk], 0)] + [(side_refs[xo], zk * cap) for xo in range(nx - 1)]
    return found + [(ref, 0) for ref in far_refs]


def fence_kernel(out_ref):
    out_ref[...] = jnp.zeros_like(out_ref)


def gather_kernel(n, nx, cap, count, ny, place_ref, *refs):
    found = found_x(n, nx, cap, refs[:count])
    meta_ref, *part_refs = refs[count : count + 1 + ny]
    rows_ref, w_ref, metas_ref = refs[count + 1 + ny :]
    toks = meta_ref.shape[1]
    d = rows_ref.shape[1]
    slot = lax.broadcasted_iota(jnp.int32, (cap, toks), 0).astype(F32)
    for j, (ref, at) in enumerate(found):
        row = j * cap
        rows_ref[row : row + cap, :] = ref[at : at + cap, 0:d]
        if j:
            metas_ref[j] = ref[at : at + 2 * n, d:]
        else:
            metas_ref[j] = meta_ref[...]
        meta = metas_ref[j].astype(F32)
        picked = jnp.where(slot == meta[j : j + 1, :], meta[n + j : n + j + 1, :], 0.0)
        total = jnp.sum(picked, axis=1, keepdims=True)
        w_ref[row : row + cap, :] = jnp.broadcast_to(total, (cap, w_ref.shape[1]))
    width = part_refs[0].shape[1]
    for yo, ref in enumerate(part_refs):
        at = pl.multiple_of((place_ref[0] ^ yo) * width, 128)
        ref[...] = rows_ref[:, pl.ds(at, width)]


def forward_kernel(rows_ref, w_ref, gate_ref, up_ref, hidden_ref, pa_ref, pb_ref):
    a = jnp.dot(rows_ref[...], gate_ref[0], preferred_element_type=F32)
    b = jnp.dot(rows_ref[...], up_ref[0], preferred_element_type=F32)
    w = w_ref[:, 0:1]
    sig = jax.nn.sigmoid(a)
    silu = a * sig
    hidden_ref[...] = (silu * b).astype(BF16)
    pa_ref[...] = w * b * sig * (1.0 + a * (1.0 - sig))
    pb_ref[...] = w * silu


def back_kernel(count, steps, me_ref, *refs):
    del me_ref
    y_refs = refs[:count]
    hidden_ref, pa_ref, pb_ref, down_ref, gate_ref, up_ref, grads_ref, score_ref, *refs = refs[count:]
    out_refs, (rows_ref, part_ref, all_ref) = refs[:-3], refs[-3:]
    step = pl.program_id(0)
    tile = down_ref.shape[1]
    feats = gate_ref.shape[1]

    @pl.when(step == 0)
    def _():
        row = 0
        for ref in y_refs:
            rows_ref[row : row + ref.shape[0], :] = ref[...]
            row += ref.shape[0]
        part_ref[...] = jnp.zeros_like(part_ref)

    @pl.when(step < steps)
    def _():
        back = lax.dot_general(rows_ref[...], down_ref[0], NT, preferred_element_type=F32)
        da = (back * pa_ref[...]).astype(BF16)
        db = (back * pb_ref[...]).astype(BF16)
        grads_ref[0] = da
        grads_ref[1] = db
        at = pl.ds(pl.multiple_of(step * tile, tile), tile)
        all_ref[0, :, at] = da
        all_ref[1, :, at] = db
        prod = back * hidden_ref[...].astype(F32)
        part = part_ref[...]
        for c in range(prod.shape[1] // 128):
            part = part + prod[:, c * 128 : (c + 1) * 128]
        part_ref[...] = part

    @pl.when(step == steps - 1)
    def _():
        total = jnp.sum(jnp.transpose(part_ref[...]), axis=0, keepdims=True)
        shape = score_ref.shape
        top = lax.broadcasted_iota(jnp.int32, shape, 0) == 0
        score_ref[...] = jnp.where(top, jnp.broadcast_to(total, shape), 0.0).astype(BF16)

    @pl.when(step >= steps)
    def _():
        val = lax.dot_general(gate_ref[0], all_ref[0], NT, preferred_element_type=F32)
        val = val + lax.dot_general(up_ref[0], all_ref[1], NT, preferred_element_type=F32)
        val = val.astype(BF16)
        for i, out in enumerate(out_refs):

            @pl.when(step == steps + i)
            def _():
                out[0:feats, :] = val
                out[feats:, :] = score_ref[...]


def rowgrad_kernel(places, dest_ref, grads_ref, score_ref, gate_ref, up_ref, *out_refs):
    del dest_ref
    size = gate_ref.shape[1]
    val = lax.dot_general(gate_ref[0], grads_ref[0], NT, preferred_element_type=F32)
    val = val + lax.dot_general(up_ref[0], grads_ref[1], NT, preferred_element_type=F32)
    val = val.astype(BF16)
    for i, (out, at) in enumerate(places):

        @pl.when(pl.program_id(0) == i)
        def _():
            out_refs[out][at : at + size, :] = val
            out_refs[out][at + size : at + size + 16, :] = score_ref[...]


def second_back_kernel(nx, size, came_ref, *refs):
    for i in range(nx - 1):
        out = refs[nx - 1 + i]
        out[0:size, :] = refs[i][...]
        out[size:, :] = came_ref[(i + 1) * size : (i + 2) * size, :]


def combine_kernel(n, cap, feats, parts, more, last, me_ref, ids_ref, metas_ref, *refs):
    me = me_ref[0]
    rows = n * cap
    toks = metas_ref.shape[2]
    metas = [metas_ref[j].astype(F32) for j in range(n)]
    if more:
        total = refs[-4][...].astype(F32)
        gg = [refs[-3][0], refs[-3][1]]
    else:
        total = jnp.zeros((feats, n * toks), F32)
        gg = [jnp.zeros((16, toks), F32)] * 2
    out_ref, gates_ref = refs[-2:]
    row = lax.broadcasted_iota(jnp.int32, (rows, n * toks), 0).astype(F32)
    for k, which, at in parts:
        wanted = []
        for j in range(n):
            code = metas[j][j ^ k : (j ^ k) + 1, :]
            wanted.append(jnp.where(code >= 0.0, code + float((j ^ k) * cap), -1.0))
        wanted = jnp.concatenate(wanted, axis=1)
        pick = (row == wanted).astype(F32).astype(BF16)
        got = refs[which][at : at + feats, :]
        total = total + jnp.dot(got, pick, preferred_element_type=F32)
        got = refs[which][at + feats : at + feats + 16, :]
        score = jnp.dot(got, pick[:, 0:toks], preferred_element_type=F32)
        gg = [gg[c] + jnp.where(ids_ref[c : c + 1, :] == (me ^ k), score, 0.0) for c in (0, 1)]
    if not last:
        out_ref[...] = total.astype(BF16)
        gates_ref[0] = gg[0]
        gates_ref[1] = gg[1]
        return
    for j in range(n):
        place = pl.multiple_of((me ^ j) * toks, toks)
        out_ref[:, pl.ds(place, toks)] = total[:, j * toks : (j + 1) * toks].astype(BF16)
    gates_ref[...] = jnp.concatenate([gg[0][0:1], gg[1][0:1]], axis=0).astype(BF16)


def first_weights_kernel(rows, core_ref, x_ref, x_came_ref, g_ref, g_came_ref, out_ref, mark_ref, xt_ref, both_ref):
    block = xt_ref.shape[0]

    @pl.when(pl.program_id(0) == 0)
    def _():
        mark_ref[...] = jnp.zeros_like(mark_ref)
        take_halves(rows, block, core_ref, x_ref, x_came_ref, xt_ref, 0)

    for half in range(2):
        both_ref[0:rows] = g_ref[half]
        both_ref[rows:] = g_came_ref[half]
        out_ref[half] = jnp.dot(xt_ref[...], both_ref[...], preferred_element_type=F32).astype(BF16)


def take_halves(rows, block, core_ref, x_ref, x_came_ref, xt_ref, at):
    @pl.when(core_ref[0] == 0)
    def _():
        xt_ref[:, at : at + rows] = x_ref[:, :block].T
        xt_ref[:, at + rows : at + 2 * rows] = x_came_ref[:, :block].T

    @pl.when(core_ref[0] != 0)
    def _():
        xt_ref[:, at : at + rows] = x_ref[:, block:].T
        xt_ref[:, at + rows : at + 2 * rows] = x_came_ref[:, block:].T


def rest_weights_kernel(rows, others, core_ref, *refs):
    x_refs, refs = refs[: 2 * others], refs[2 * others :]
    g_refs, part_ref = refs[: 2 * others], refs[2 * others]
    gate_ref, up_ref, mark_ref, xt_ref, all_ref = refs[2 * others + 1 :]
    block = xt_ref.shape[0]

    @pl.when(pl.program_id(0) == 0)
    def _():
        mark_ref[...] = jnp.zeros_like(mark_ref)
        for i in range(others):
            take_halves(rows, block, core_ref, x_refs[2 * i], x_refs[2 * i + 1], xt_ref, 2 * i * rows)

    for half, out in ((0, gate_ref), (1, up_ref)):
        for i, ref in enumerate(g_refs):
            all_ref[i * rows : (i + 1) * rows] = ref[half]
        total = jnp.dot(xt_ref[...], all_ref[...], preferred_element_type=F32)
        total = total + part_ref[half].astype(F32)
        out[0] = (total * (1.0 / (2 * others + 2))).astype(BF16)


def local(tokens, cotangent, gates, expert_ids, gate_w, up_w, down_w):
    toks, d = tokens.shape
    top = expert_ids.shape[1]
    h = gate_w.shape[2]
    n = lax.axis_size("expert")
    ndp = lax.axis_size("dp")
    nz = 4
    nx = n // nz
    ny = ndp // 2
    cap = -(-(3 * toks * top // (2 * n)) // 16) * 16
    rows = n * cap
    feats = d // n
    size = feats + 16
    block = d // ndp
    wide = d + toks
    me = lax.axis_index("expert").astype(jnp.int32)
    my_dp = lax.axis_index("dp").astype(jnp.int32)
    me_arr = me.reshape(1)
    my_y, my_core = (my_dp // 2).reshape(1), (my_dp % 2).reshape(1)
    ids_t = expert_ids.T
    gates_t = gates.T
    any_space = pl.BlockSpec(memory_space=pl.ANY)

    def swap(v, k):
        return lax.ppermute(v, "expert", [(i, i ^ k) for i in range(n)])

    def swap_dp(v, q):
        return lax.ppermute(v, "dp", [(i, i ^ q) for i in range(ndp)])

    def shape(*dims, dtype=BF16):
        return jax.ShapeDtypeStruct(dims, dtype)

    previous = []

    def run(body, name, outs, args, in_specs, out_specs, after=(), grid=(), scalars=0, scratch=(), weight=LONG, mib=48, alias=None):
        waits = [*after, *previous]
        first = len(args)

        def trimmed(*refs):
            body(*refs[:first], *refs[first + len(waits) :])

        made = pl.pallas_call(
            trimmed,
            grid_spec=pltpu.PrefetchScalarGridSpec(
                num_scalar_prefetch=scalars,
                grid=grid,
                in_specs=[*in_specs, *[any_space] * len(waits)],
                out_specs=out_specs,
                scratch_shapes=scratch,
            ),
            out_shape=outs,
            compiler_params=params(mib),
            input_output_aliases=alias or {},
            cost_estimate=pl.CostEstimate(flops=weight, bytes_accessed=1, transcendentals=0),
            name=name,
        )(*args, *waits)
        previous[:] = [min(made, key=lambda v: v.size)]
        return made

    whole = lambda dims: pl.BlockSpec(dims, lambda *_: (0,) * len(dims))

    def call(body, name, outs, args, after=(), scalars=0, **kinds):
        in_specs = [smem()] * scalars + vmem(len(args) - scalars)
        return run(body, name, outs, args, in_specs, vmem(len(outs)), after, **kinds)

    def hold(values, after=(), weight=LONG):
        outs = [jax.ShapeDtypeStruct(v.shape, v.dtype) for v in values]
        count = len(values)
        alias = {i: i for i in range(count)}
        spaces = [any_space] * count
        return run(lambda *_: None, "hold", outs, values, spaces, spaces, after, weight=weight, alias=alias)

    def fence(after):
        call(fence_kernel, "fence", [shape(8, 128, dtype=F32)], [], after)

    sources = [ids_t, gates_t, tokens, cotangent]
    outs = (
        [shape(2 * n, toks), shape(nx * cap, wide), shape(cap, d)]
        + [shape(cap, wide)] * (nx - 1)
        + [shape(nz // 2 * cap, d)] * (2 * nx - 2)
    )
    x_all = swap(tokens, 2 * nx)
    meta, x_near, x_own, *made = run(
        functools.partial(prep_kernel, n, nx, cap),
        "prep",
        outs,
        [me_arr, *sources],
        [smem()] + [pl.BlockSpec(memory_space=pltpu.HBM)] * len(sources),
        vmem(len(outs)),
        scratch=[pltpu.VMEM(v.shape, v.dtype) for v in sources]
        + [pltpu.SemaphoreType.DMA((len(sources),))],
        mib=59,
    )
    x_side, y_side = made[: nx - 1], made[nx - 1 :]
    x_near = swap(x_near, nx)
    meta_all = swap(meta, 2 * nx)
    y_side = [swap(v, i // 2 + 1) for i, v in enumerate(y_side)]
    y_sent = call(
        functools.partial(second_kernel, n, nx, cap),
        "second",
        [shape(nx * cap, d)] * nz,
        [meta, cotangent, *y_side],
        weight=1,
        mib=59,
    )
    made = call(
        functools.partial(third_kernel, n, nx, cap),
        "third",
        [shape((nz - 1) * cap, wide)] * (nx - 1) + [shape(cap, wide)] * (1 + nx),
        [x_all, meta_all, x_near, *x_side],
        mib=59,
    )
    x_side = [swap(v, xo) for xo, v in enumerate(made[: nx - 1], 1)]
    x_mid, x_passed = made[nx - 1], made[nx:]
    x_far = [swap(v, nx + xo) for xo, v in enumerate(x_passed)]
    y_mid = swap(y_sent[2], 2 * nx)
    got_x = [x_own, x_near, x_mid, *x_side, *x_far]
    y_near = swap(y_sent[1], nx)
    y_far = swap(hold([y_sent[3]], [*x_far, y_mid])[0], 3 * nx)

    tile = 256
    steps = h // tile
    column = pl.BlockSpec((rows, tile), lambda i: (0, i))
    *x_parts, x_rows, row_w, metas = call(
        functools.partial(gather_kernel, n, nx, cap, len(got_x), ny),
        "gather",
        [shape(rows, 2 * block)] * ny
        + [shape(rows, d), shape(rows, 128, dtype=F32), shape(n, 2 * n, toks)],
        [my_y, *got_x, meta],
        scalars=1,
        mib=59,
        weight=1,
    )
    x_own_came = swap_dp(x_parts[0], 1)
    x_parts = [x_parts[0]] + [swap_dp(v, 2 * yo) for yo, v in enumerate(x_parts[1:], 1)]
    hidden, pa, pb = run(
        forward_kernel,
        "forward",
        [shape(rows, h), shape(rows, h, dtype=F32), shape(rows, h, dtype=F32)],
        [x_rows, row_w, gate_w, up_w],
        [whole((rows, d)), whole((rows, 128))]
        + [pl.BlockSpec((1, d, tile), lambda i: (0, 0, i))] * 2,
        [column] * 3,
        grid=(steps,),
        weight=1,
    )
    fence([y_near])
    got_y = [y_sent[0], y_near, y_mid, y_far]
    first_sent = list(range(n - nx + 1, n))
    held = lambda i: jnp.minimum(i, steps - 1)
    column_b = pl.BlockSpec((rows, tile), lambda i, _: (0, held(i)))

    def first_owner(i, me_ref):
        k = jnp.maximum(i - steps, 0) + first_sent[0]
        return (0, k ^ me_ref[0], 0)

    out_spec = pl.BlockSpec((1, feats, h), first_owner)
    grads, score, *sent = run(
        functools.partial(back_kernel, len(got_y), steps),
        "back",
        [shape(2, rows, h), shape(16, rows)] + [shape(size, rows)] * (nx - 1),
        [me_arr, *got_y, hidden, pa, pb, down_w, gate_w, up_w],
        [whole(v.shape) for v in got_y]
        + [column_b] * 3
        + [pl.BlockSpec((1, tile, d), lambda i, _: (0, held(i), 0)), out_spec, out_spec],
        [pl.BlockSpec((2, rows, tile), lambda i, _: (0, 0, held(i)))]
        + [whole((16, rows))]
        + [whole((size, rows))] * (nx - 1),
        after=[x_own_came],
        grid=(steps + nx - 1,),
        scalars=1,
        scratch=[
            pltpu.VMEM((rows, d), BF16),
            pltpu.VMEM((rows, 128), F32),
            pltpu.VMEM((2, rows, h), BF16),
        ],
        weight=1,
        mib=59,
    )
    g_own_came = swap_dp(grads, 1)
    g_parts = [grads] + [swap_dp(grads, 2 * yo) for yo in range(1, ny)]

    def rowgrads(places, outs, after=(), weight=1):
        def owner(i, me_ref):
            k = jnp.int32(places[0][0])
            for at, (other, _, _) in enumerate(places):
                k = jnp.where(i == at, other, k)
            return (0, k ^ me_ref[0], 0)

        spec = pl.BlockSpec((1, feats, h), owner)
        fixed = whole
        return run(
            functools.partial(rowgrad_kernel, [(out, at) for _, out, at in places]),
            "rowgrad",
            [shape(size * many, rows) for many in outs],
            [me_arr, grads, score, gate_w, up_w],
            [fixed((2, rows, h)), fixed((16, rows)), spec, spec],
            [fixed((size * many, rows)) for many in outs],
            after,
            grid=(len(places),),
            scalars=1,
            weight=weight,
            mib=59,
        )

    far = list(range(n - nx, n))
    mids = list(range(2 * nx, n - nx))
    straight = {}

    def send(ks, values):
        for k, v in zip(ks, values):
            straight[k] = swap(v, k)

    sent = hold(sent, weight=1)
    send(first_sent, sent)
    near, sent = rowgrads(
        [(nx + xo, 0, xo * size) for xo in range(nx)] + [(far[0], 1, 0)],
        [nx, 1],
        x_parts[1:],
        weight=LONG,
    )
    near = swap(near, nx)
    send(far[:1], [sent])
    tile_w = 256
    part_spec = pl.BlockSpec((2, block, tile_w), lambda i: (0, 0, i))
    column_w = pl.BlockSpec((2, rows, tile_w), lambda i: (0, 0, i))
    x_spec = whole((rows, 2 * block))
    w_part, _ = run(
        functools.partial(first_weights_kernel, rows),
        "weights",
        [shape(2, block, h), shape(8, 128, dtype=F32)],
        [my_core, x_parts[0], x_own_came, grads, g_own_came],
        [smem(), x_spec, x_spec, column_w, column_w],
        [part_spec, whole((8, 128))],
        grid=(h // tile_w,),
        scratch=[pltpu.VMEM((block, 2 * rows), BF16), pltpu.VMEM((2 * rows, tile_w), BF16)],
    )
    x_came = [swap_dp(v, 1) for v in x_parts[1:]]
    last = mids[::-1]
    own, *sent = rowgrads(
        [(k, i, 0) for i, k in enumerate([0, *range(1, nx), *last])],
        [1] * (nx + len(last)),
        x_came,
        weight=LONG,
    )
    by_column, sent = sent[: nx - 1], sent[nx - 1 :]
    send(last, sent)

    g_came = [swap_dp(v, 1) for v in g_parts[1:]]
    fence(g_parts[1:])

    sent = call(
        functools.partial(second_back_kernel, nx, size),
        "second_back",
        [shape(2 * size, rows)] * (nx - 1),
        [near, *by_column],
        [straight[k] for k in far[1:]],
    )
    columns = [swap(v, xo) for xo, v in enumerate(sent, 1)]

    sum_shapes = [shape(feats, n * toks), shape(2, 16, toks, dtype=F32)]

    def combine(parts, refs, carried, outs, final):
        return call(
            functools.partial(combine_kernel, n, cap, feats, parts, bool(carried), final),
            "combine",
            outs,
            [me_arr, ids_t, metas, *refs, *carried],
            scalars=1,
        )

    parts = [(0, 0, 0), (nx, 1, 0)] + [(k, i, 0) for i, k in enumerate(far, 2)]
    sums = combine(
        parts,
        [own, near, *[straight[k] for k in far]],
        [],
        sum_shapes,
        False,
    )

    others = ny - 1
    out_spec = pl.BlockSpec((1, block, tile_w), lambda i: (0, 0, i))
    pairs = lambda ours, theirs: [v for both in zip(ours, theirs) for v in both]
    grad_gate_w, grad_up_w, _ = run(
        functools.partial(rest_weights_kernel, rows, others),
        "weights_rest",
        [shape(1, block, h)] * 2 + [shape(8, 128, dtype=F32)],
        [my_core, *pairs(x_parts[1:], x_came), *pairs(g_parts[1:], g_came), w_part],
        [smem()] + [x_spec] * (2 * others) + [column_w] * (2 * others) + [part_spec],
        [out_spec, out_spec, whole((8, 128))],
        grid=(h // tile_w,),
        scratch=[
            pltpu.VMEM((block, 2 * others * rows), BF16),
            pltpu.VMEM((2 * others * rows, tile_w), BF16),
        ],
    )

    parts = []
    for i in range(nx - 1):
        parts += [(i + 1, i, 0), (nx + i + 1, i, size)]
    sums = combine(parts, columns, sums, sum_shapes, False)
    summed, gg = combine(
        [(k, i, 0) for i, k in enumerate(last)],
        [straight[k] for k in last],
        sums,
        [shape(feats, n * toks), shape(2, toks)],
        True,
    )
    return summed.T, grad_gate_w, grad_up_w, gg.T


def solution(mesh):
    placed = (
        P(("dp", "expert"), None),
        P(("dp", "expert"), None),
        P(("dp", "expert"), None),
        P(("dp", "expert"), None),
        P("expert", None, None),
        P("expert", None, None),
        P("expert", None, None),
    )
    return jax.shard_map(
        local,
        mesh=mesh,
        in_specs=placed,
        out_specs=(
            P("dp", "expert"),
            P("expert", "dp", None),
            P("expert", "dp", None),
            P(("dp", "expert"), None),
        ),
        check_vma=False,
    )
```

```python
import functools

import jax
import jax.numpy as jnp
from jax import lax
from jax.experimental import pallas as pl
from jax.experimental.pallas import tpu as pltpu
from jax.sharding import PartitionSpec as P

F32 = jnp.float32
BF16 = jnp.bfloat16
NT = (((1,), (1,)), ((), ()))
TN = (((0,), (0,)), ((), ()))


def params(mib=48):
    return pltpu.CompilerParams(vmem_limit_bytes=mib << 20)


def vmem(count):
    return [pl.BlockSpec(memory_space=pltpu.VMEM)] * count


def smem():
    return pl.BlockSpec(memory_space=pltpu.SMEM)


LONG = 1 << 40


def pick_rows(cap, code, meta, tokens, dest):
    toks, d = tokens.shape
    slot = lax.broadcasted_iota(jnp.int32, (cap, toks), 0).astype(F32)
    for j, ref, at in dest:
        pick = (slot == code[j : j + 1, :]).astype(F32).astype(BF16)
        chosen = jnp.dot(pick, tokens, preferred_element_type=F32).astype(BF16)
        ref[at : at + cap, 0:d] = chosen
        if ref.shape[1] > d:
            add_routing(ref, at, cap, d, meta)


def add_routing(ref, at, count, d, meta):
    ref[at : at + count, d:] = jnp.zeros((count, meta.shape[1]), BF16)
    ref[at : at + meta.shape[0], d:] = meta


def prep_kernel(n, nx, cap, me_ref, *refs):
    sources, meta_ref, out_refs = refs[:4], refs[4], refs[5:-5]
    held, sems = refs[-5:-1], refs[-1]
    copies = [
        pltpu.make_async_copy(src, dst, sems.at[i])
        for i, (src, dst) in enumerate(zip(sources, held))
    ]
    for copy in copies:
        copy.start()
    ids_ref, gates_ref, tok_ref, cot_ref = held
    copies[0].wait()
    copies[1].wait()
    toks = tok_ref.shape[0]
    nz = n // nx
    expert = lax.broadcasted_iota(jnp.int32, (n, toks), 0) ^ me_ref[0]
    first = ids_ref[0:1, :] == expert
    second = ids_ref[1:2, :] == expert
    count = (first | second).astype(F32)
    before = (
        lax.broadcasted_iota(jnp.int32, (toks, toks), 0)
        < lax.broadcasted_iota(jnp.int32, (toks, toks), 1)
    ).astype(F32)
    position = jnp.dot(count.astype(BF16), before.astype(BF16), preferred_element_type=F32)
    code = jnp.where(first | second, position, -1.0)
    gates = gates_ref[...].astype(F32)
    weight = jnp.where(first, gates[0:1, :], 0.0) + jnp.where(second, gates[1:2, :], 0.0)
    meta = jnp.concatenate([code, weight], axis=0).astype(BF16)
    meta_ref[...] = meta
    halves = 2 * (nx - 1)
    near_ref, rest, y_refs = out_refs[0], out_refs[1:-halves], out_refs[-halves:]
    copies[2].wait()
    tokens = tok_ref[...]
    near = [(nx + xo, near_ref, xo * cap) for xo in range(nx)]
    pick_rows(cap, code, meta, tokens, near + [(j, ref, 0) for j, ref in enumerate(rest)])
    by_column = [
        (zk * nx + xo, y_refs[2 * xo - 2 + zk // 2], zk % 2 * cap) for zk in range(nz) for xo in range(1, nx)
    ]
    copies[3].wait()
    pick_rows(cap, code, meta, cot_ref[...], by_column)


def second_kernel(n, nx, cap, meta_ref, cot_ref, *refs):
    nz = n // nx
    came, y_refs = refs[: 2 * nx - 2], refs[2 * nx - 2 :]
    meta = meta_ref[...]
    own = [(zk * nx, y_refs[zk], 0) for zk in range(nz)]
    pick_rows(cap, meta.astype(F32)[0:n, :], meta, cot_ref[...], own)
    for xo in range(1, nx):
        for zk in range(nz):
            at = zk % 2 * cap
            y_refs[zk][xo * cap : (xo + 1) * cap, :] = came[2 * xo - 2 + zk // 2][at : at + cap, :]


def third_kernel(n, nx, cap, all_ref, meta_ref, near_ref, *refs):
    own, x_refs, here_ref, pass_refs = refs[: nx - 1], refs[nx - 1 : 2 * nx - 2], refs[2 * nx - 2], refs[2 * nx - 1 :]
    meta = meta_ref[...]
    dest = [(2 * nx, here_ref, 0)] + [(2 * nx + xo, x_refs[xo - 1], 2 * cap) for xo in range(1, nx)]
    dest += [(3 * nx + xo, pass_refs[xo], 0) for xo in range(nx)]
    pick_rows(cap, meta.astype(F32)[0:n, :], meta, all_ref[...], dest)
    for xo in range(1, nx):
        x_refs[xo - 1][0:cap, :] = own[xo - 1][...]
        x_refs[xo - 1][cap : 2 * cap, :] = near_ref[xo * cap : (xo + 1) * cap, :]


def found_x(n, nx, cap, refs):
    nz = n // nx
    z_refs, side_refs, far_refs = refs[: nz - 1], refs[nz - 1 : nz + nx - 2], refs[nz + nx - 2 :]
    found = []
    for zk in range(nz - 1):
        found += [(z_refs[zk], 0)] + [(side_refs[xo], zk * cap) for xo in range(nx - 1)]
    return found + [(ref, 0) for ref in far_refs]


def fence_kernel(out_ref):
    out_ref[...] = jnp.zeros_like(out_ref)


def gather_kernel(n, nx, cap, count, ny, place_ref, *refs):
    found = found_x(n, nx, cap, refs[:count])
    meta_ref, *part_refs = refs[count : count + 1 + ny]
    rows_ref, w_ref, metas_ref = refs[count + 1 + ny :]
    toks = meta_ref.shape[1]
    d = rows_ref.shape[1]
    slot = lax.broadcasted_iota(jnp.int32, (cap, toks), 0).astype(F32)
    for j, (ref, at) in enumerate(found):
        row = j * cap
        rows_ref[row : row + cap, :] = ref[at : at + cap, 0:d]
        if j:
            metas_ref[j] = ref[at : at + 2 * n, d:]
        else:
            metas_ref[j] = meta_ref[...]
        meta = metas_ref[j].astype(F32)
        picked = jnp.where(slot == meta[j : j + 1, :], meta[n + j : n + j + 1, :], 0.0)
        total = jnp.sum(picked, axis=1, keepdims=True)
        w_ref[row : row + cap, :] = jnp.broadcast_to(total, (cap, w_ref.shape[1]))
    width = part_refs[0].shape[1]
    for yo, ref in enumerate(part_refs):
        at = pl.multiple_of((place_ref[0] ^ yo) * width, 128)
        ref[...] = rows_ref[:, pl.ds(at, width)]


def forward_kernel(rows_ref, w_ref, gate_ref, up_ref, hidden_ref, pa_ref, pb_ref):
    a = jnp.dot(rows_ref[...], gate_ref[0], preferred_element_type=F32)
    b = jnp.dot(rows_ref[...], up_ref[0], preferred_element_type=F32)
    w = w_ref[:, 0:1]
    sig = jax.nn.sigmoid(a)
    silu = a * sig
    hidden_ref[...] = (silu * b).astype(BF16)
    pa_ref[...] = w * b * sig * (1.0 + a * (1.0 - sig))
    pb_ref[...] = w * silu


def back_kernel(count, steps, me_ref, *refs):
    del me_ref
    y_refs = refs[:count]
    hidden_ref, pa_ref, pb_ref, down_ref, gate_ref, up_ref, grads_ref, score_ref, *refs = refs[count:]
    out_refs, (rows_ref, part_ref, all_ref) = refs[:-3], refs[-3:]
    step = pl.program_id(0)
    tile = down_ref.shape[1]
    feats = gate_ref.shape[1]

    @pl.when(step == 0)
    def _():
        row = 0
        for ref in y_refs:
            rows_ref[row : row + ref.shape[0], :] = ref[...]
            row += ref.shape[0]
        part_ref[...] = jnp.zeros_like(part_ref)

    @pl.when(step < steps)
    def _():
        back = lax.dot_general(rows_ref[...], down_ref[0], NT, preferred_element_type=F32)
        da = (back * pa_ref[...]).astype(BF16)
        db = (back * pb_ref[...]).astype(BF16)
        grads_ref[0] = da
        grads_ref[1] = db
        at = pl.ds(pl.multiple_of(step * tile, tile), tile)
        all_ref[0, :, at] = da
        all_ref[1, :, at] = db
        prod = back * hidden_ref[...].astype(F32)
        part = part_ref[...]
        for c in range(prod.shape[1] // 128):
            part = part + prod[:, c * 128 : (c + 1) * 128]
        part_ref[...] = part

    @pl.when(step == steps - 1)
    def _():
        total = jnp.sum(jnp.transpose(part_ref[...]), axis=0, keepdims=True)
        shape = score_ref.shape
        top = lax.broadcasted_iota(jnp.int32, shape, 0) == 0
        score_ref[...] = jnp.where(top, jnp.broadcast_to(total, shape), 0.0).astype(BF16)

    @pl.when(step >= steps)
    def _():
        val = lax.dot_general(gate_ref[0], all_ref[0], NT, preferred_element_type=F32)
        val = val + lax.dot_general(up_ref[0], all_ref[1], NT, preferred_element_type=F32)
        val = val.astype(BF16)
        for i, out in enumerate(out_refs):

            @pl.when(step == steps + i)
            def _():
                out[0:feats, :] = val
                out[feats:, :] = score_ref[...]


def rowgrad_kernel(places, dest_ref, grads_ref, score_ref, gate_ref, up_ref, *out_refs):
    del dest_ref
    size = gate_ref.shape[1]
    val = lax.dot_general(gate_ref[0], grads_ref[0], NT, preferred_element_type=F32)
    val = val + lax.dot_general(up_ref[0], grads_ref[1], NT, preferred_element_type=F32)
    val = val.astype(BF16)
    for i, (out, at) in enumerate(places):

        @pl.when(pl.program_id(0) == i)
        def _():
            out_refs[out][at : at + size, :] = val
            out_refs[out][at + size : at + size + 16, :] = score_ref[...]


def second_back_kernel(nx, size, came_ref, *refs):
    for i in range(nx - 1):
        out = refs[nx - 1 + i]
        out[0:size, :] = refs[i][...]
        out[size:, :] = came_ref[(i + 1) * size : (i + 2) * size, :]


def combine_kernel(n, cap, feats, parts, more, last, me_ref, ids_ref, metas_ref, *refs):
    me = me_ref[0]
    rows = n * cap
    toks = metas_ref.shape[2]
    metas = [metas_ref[j].astype(F32) for j in range(n)]
    if more:
        total = refs[-4][...].astype(F32)
        gg = [refs[-3][0], refs[-3][1]]
    else:
        total = jnp.zeros((feats, n * toks), F32)
        gg = [jnp.zeros((16, toks), F32)] * 2
    out_ref, gates_ref = refs[-2:]
    row = lax.broadcasted_iota(jnp.int32, (rows, n * toks), 0).astype(F32)
    for k, which, at in parts:
        wanted = []
        for j in range(n):
            code = metas[j][j ^ k : (j ^ k) + 1, :]
            wanted.append(jnp.where(code >= 0.0, code + float((j ^ k) * cap), -1.0))
        wanted = jnp.concatenate(wanted, axis=1)
        pick = (row == wanted).astype(F32).astype(BF16)
        got = refs[which][at : at + feats, :]
        total = total + jnp.dot(got, pick, preferred_element_type=F32)
        got = refs[which][at + feats : at + feats + 16, :]
        score = jnp.dot(got, pick[:, 0:toks], preferred_element_type=F32)
        gg = [gg[c] + jnp.where(ids_ref[c : c + 1, :] == (me ^ k), score, 0.0) for c in (0, 1)]
    if not last:
        out_ref[...] = total.astype(BF16)
        gates_ref[0] = gg[0]
        gates_ref[1] = gg[1]
        return
    for j in range(n):
        place = pl.multiple_of((me ^ j) * toks, toks)
        out_ref[:, pl.ds(place, toks)] = total[:, j * toks : (j + 1) * toks].astype(BF16)
    gates_ref[...] = jnp.concatenate([gg[0][0:1], gg[1][0:1]], axis=0).astype(BF16)


def first_weights_kernel(rows, core_ref, x_ref, x_came_ref, g_ref, g_came_ref, out_ref, mark_ref, xt_ref, both_ref):
    block = xt_ref.shape[0]

    @pl.when(pl.program_id(0) == 0)
    def _():
        mark_ref[...] = jnp.zeros_like(mark_ref)
        take_halves(rows, block, core_ref, x_ref, x_came_ref, xt_ref, 0)

    for half in range(2):
        both_ref[0:rows] = g_ref[half]
        both_ref[rows:] = g_came_ref[half]
        out_ref[half] = jnp.dot(xt_ref[...], both_ref[...], preferred_element_type=F32).astype(BF16)


def take_halves(rows, block, core_ref, x_ref, x_came_ref, xt_ref, at):
    @pl.when(core_ref[0] == 0)
    def _():
        xt_ref[:, at : at + rows] = x_ref[:, :block].T
        xt_ref[:, at + rows : at + 2 * rows] = x_came_ref[:, :block].T

    @pl.when(core_ref[0] != 0)
    def _():
        xt_ref[:, at : at + rows] = x_ref[:, block:].T
        xt_ref[:, at + rows : at + 2 * rows] = x_came_ref[:, block:].T


def rest_weights_kernel(rows, others, core_ref, *refs):
    x_refs, refs = refs[: 2 * others], refs[2 * others :]
    g_refs, part_ref = refs[: 2 * others], refs[2 * others]
    gate_ref, up_ref, mark_ref, xt_ref, all_ref = refs[2 * others + 1 :]
    block = xt_ref.shape[0]

    @pl.when(pl.program_id(0) == 0)
    def _():
        mark_ref[...] = jnp.zeros_like(mark_ref)
        for i in range(others):
            take_halves(rows, block, core_ref, x_refs[2 * i], x_refs[2 * i + 1], xt_ref, 2 * i * rows)

    for half, out in ((0, gate_ref), (1, up_ref)):
        for i, ref in enumerate(g_refs):
            all_ref[i * rows : (i + 1) * rows] = ref[half]
        total = jnp.dot(xt_ref[...], all_ref[...], preferred_element_type=F32)
        total = total + part_ref[half].astype(F32)
        out[0] = (total * (1.0 / (2 * others + 2))).astype(BF16)


def local(tokens, cotangent, gates, expert_ids, gate_w, up_w, down_w):
    toks, d = tokens.shape
    top = expert_ids.shape[1]
    h = gate_w.shape[2]
    n = lax.axis_size("expert")
    ndp = lax.axis_size("dp")
    nz = 4
    nx = n // nz
    ny = ndp // 2
    cap = -(-(3 * toks * top // (2 * n)) // 16) * 16
    rows = n * cap
    feats = d // n
    size = feats + 16
    block = d // ndp
    wide = d + toks
    me = lax.axis_index("expert").astype(jnp.int32)
    my_dp = lax.axis_index("dp").astype(jnp.int32)
    me_arr = me.reshape(1)
    my_y, my_core = (my_dp // 2).reshape(1), (my_dp % 2).reshape(1)
    ids_t = expert_ids.T
    gates_t = gates.T
    any_space = pl.BlockSpec(memory_space=pl.ANY)

    def swap(v, k):
        return lax.ppermute(v, "expert", [(i, i ^ k) for i in range(n)])

    def swap_dp(v, q):
        return lax.ppermute(v, "dp", [(i, i ^ q) for i in range(ndp)])

    def shape(*dims, dtype=BF16):
        return jax.ShapeDtypeStruct(dims, dtype)

    previous = []

    def run(body, name, outs, args, in_specs, out_specs, after=(), grid=(), scalars=0, scratch=(), weight=LONG, mib=48, alias=None):
        waits = [*after, *previous]
        first = len(args)

        def trimmed(*refs):
            body(*refs[:first], *refs[first + len(waits) :])

        made = pl.pallas_call(
            trimmed,
            grid_spec=pltpu.PrefetchScalarGridSpec(
                num_scalar_prefetch=scalars,
                grid=grid,
                in_specs=[*in_specs, *[any_space] * len(waits)],
                out_specs=out_specs,
                scratch_shapes=scratch,
            ),
            out_shape=outs,
            compiler_params=params(mib),
            input_output_aliases=alias or {},
            cost_estimate=pl.CostEstimate(flops=weight, bytes_accessed=1, transcendentals=0),
            name=name,
        )(*args, *waits)
        previous[:] = [min(made, key=lambda v: v.size)]
        return made

    whole = lambda dims: pl.BlockSpec(dims, lambda *_: (0,) * len(dims))

    def call(body, name, outs, args, after=(), scalars=0, **kinds):
        in_specs = [smem()] * scalars + vmem(len(args) - scalars)
        return run(body, name, outs, args, in_specs, vmem(len(outs)), after, **kinds)

    def hold(values, after=(), weight=LONG):
        outs = [jax.ShapeDtypeStruct(v.shape, v.dtype) for v in values]
        count = len(values)
        alias = {i: i for i in range(count)}
        spaces = [any_space] * count
        return run(lambda *_: None, "hold", outs, values, spaces, spaces, after, weight=weight, alias=alias)

    def fence(after):
        call(fence_kernel, "fence", [shape(8, 128, dtype=F32)], [], after)

    sources = [ids_t, gates_t, tokens, cotangent]
    outs = (
        [shape(2 * n, toks), shape(nx * cap, wide), shape(cap, d)]
        + [shape(cap, wide)] * (nx - 1)
        + [shape(nz // 2 * cap, d)] * (2 * nx - 2)
    )
    x_all = swap(tokens, 2 * nx)
    meta, x_near, x_own, *made = run(
        functools.partial(prep_kernel, n, nx, cap),
        "prep",
        outs,
        [me_arr, *sources],
        [smem()] + [pl.BlockSpec(memory_space=pltpu.HBM)] * len(sources),
        vmem(len(outs)),
        scratch=[pltpu.VMEM(v.shape, v.dtype) for v in sources]
        + [pltpu.SemaphoreType.DMA((len(sources),))],
        mib=59,
    )
    x_side, y_side = made[: nx - 1], made[nx - 1 :]
    x_near = swap(x_near, nx)
    meta_all = swap(meta, 2 * nx)
    y_side = [swap(v, i // 2 + 1) for i, v in enumerate(y_side)]
    y_sent = call(
        functools.partial(second_kernel, n, nx, cap),
        "second",
        [shape(nx * cap, d)] * nz,
        [meta, cotangent, *y_side],
        weight=1,
        mib=59,
    )
    made = call(
        functools.partial(third_kernel, n, nx, cap),
        "third",
        [shape((nz - 1) * cap, wide)] * (nx - 1) + [shape(cap, wide)] * (1 + nx),
        [x_all, meta_all, x_near, *x_side],
        mib=59,
    )
    x_side = [swap(v, xo) for xo, v in enumerate(made[: nx - 1], 1)]
    x_mid, x_passed = made[nx - 1], made[nx:]
    x_far = [swap(v, nx + xo) for xo, v in enumerate(x_passed)]
    y_mid = swap(y_sent[2], 2 * nx)
    got_x = [x_own, x_near, x_mid, *x_side, *x_far]
    y_near = swap(y_sent[1], nx)
    y_far = swap(hold([y_sent[3]], [*x_far, y_mid])[0], 3 * nx)

    tile = 256
    steps = h // tile
    column = pl.BlockSpec((rows, tile), lambda i: (0, i))
    *x_parts, x_rows, row_w, metas = call(
        functools.partial(gather_kernel, n, nx, cap, len(got_x), ny),
        "gather",
        [shape(rows, 2 * block)] * ny
        + [shape(rows, d), shape(rows, 128, dtype=F32), shape(n, 2 * n, toks)],
        [my_y, *got_x, meta],
        scalars=1,
        mib=59,
        weight=1,
    )
    x_own_came = swap_dp(x_parts[0], 1)
    x_parts = [x_parts[0]] + [swap_dp(v, 2 * yo) for yo, v in enumerate(x_parts[1:], 1)]
    hidden, pa, pb = run(
        forward_kernel,
        "forward",
        [shape(rows, h), shape(rows, h, dtype=F32), shape(rows, h, dtype=F32)],
        [x_rows, row_w, gate_w, up_w],
        [whole((rows, d)), whole((rows, 128))]
        + [pl.BlockSpec((1, d, tile), lambda i: (0, 0, i))] * 2,
        [column] * 3,
        grid=(steps,),
        weight=1,
    )
    fence([y_near])
    got_y = [y_sent[0], y_near, y_mid, y_far]
    first_sent = list(range(n - nx + 1, n))
    held = lambda i: jnp.minimum(i, steps - 1)
    column_b = pl.BlockSpec((rows, tile), lambda i, _: (0, held(i)))

    def first_owner(i, me_ref):
        k = jnp.maximum(i - steps, 0) + first_sent[0]
        return (0, k ^ me_ref[0], 0)

    out_spec = pl.BlockSpec((1, feats, h), first_owner)
    grads, score, *sent = run(
        functools.partial(back_kernel, len(got_y), steps),
        "back",
        [shape(2, rows, h), shape(16, rows)] + [shape(size, rows)] * (nx - 1),
        [me_arr, *got_y, hidden, pa, pb, down_w, gate_w, up_w],
        [whole(v.shape) for v in got_y]
        + [column_b] * 3
        + [pl.BlockSpec((1, tile, d), lambda i, _: (0, held(i), 0)), out_spec, out_spec],
        [pl.BlockSpec((2, rows, tile), lambda i, _: (0, 0, held(i)))]
        + [whole((16, rows))]
        + [whole((size, rows))] * (nx - 1),
        after=[x_own_came],
        grid=(steps + nx - 1,),
        scalars=1,
        scratch=[
            pltpu.VMEM((rows, d), BF16),
            pltpu.VMEM((rows, 128), F32),
            pltpu.VMEM((2, rows, h), BF16),
        ],
        weight=1,
        mib=59,
    )
    g_own_came = swap_dp(grads, 1)
    g_parts = [grads] + [swap_dp(grads, 2 * yo) for yo in range(1, ny)]

    def rowgrads(places, outs, after=(), weight=1):
        def owner(i, me_ref):
            k = jnp.int32(places[0][0])
            for at, (other, _, _) in enumerate(places):
                k = jnp.where(i == at, other, k)
            return (0, k ^ me_ref[0], 0)

        spec = pl.BlockSpec((1, feats, h), owner)
        fixed = whole
        return run(
            functools.partial(rowgrad_kernel, [(out, at) for _, out, at in places]),
            "rowgrad",
            [shape(size * many, rows) for many in outs],
            [me_arr, grads, score, gate_w, up_w],
            [fixed((2, rows, h)), fixed((16, rows)), spec, spec],
            [fixed((size * many, rows)) for many in outs],
            after,
            grid=(len(places),),
            scalars=1,
            weight=weight,
            mib=59,
        )

    far = list(range(n - nx, n))
    mids = list(range(2 * nx, n - nx))
    straight = {}

    def send(ks, values):
        for k, v in zip(ks, values):
            straight[k] = swap(v, k)

    sent = hold(sent, weight=1)
    send(first_sent, sent)
    near, sent = rowgrads(
        [(nx + xo, 0, xo * size) for xo in range(nx)] + [(far[0], 1, 0)],
        [nx, 1],
        x_parts[1:],
        weight=LONG,
    )
    near = swap(near, nx)
    send(far[:1], [sent])
    tile_w = 256
    part_spec = pl.BlockSpec((2, block, tile_w), lambda i: (0, 0, i))
    column_w = pl.BlockSpec((2, rows, tile_w), lambda i: (0, 0, i))
    x_spec = whole((rows, 2 * block))
    w_part, _ = run(
        functools.partial(first_weights_kernel, rows),
        "weights",
        [shape(2, block, h), shape(8, 128, dtype=F32)],
        [my_core, x_parts[0], x_own_came, grads, g_own_came],
        [smem(), x_spec, x_spec, column_w, column_w],
        [part_spec, whole((8, 128))],
        grid=(h // tile_w,),
        scratch=[pltpu.VMEM((block, 2 * rows), BF16), pltpu.VMEM((2 * rows, tile_w), BF16)],
    )
    x_came = [swap_dp(v, 1) for v in x_parts[1:]]
    last = mids[::-1]
    own, *sent = rowgrads(
        [(k, i, 0) for i, k in enumerate([0, *range(1, nx), *last])],
        [1] * (nx + len(last)),
        [*x_came, *[straight[k] for k in first_sent]],
        weight=LONG,
    )
    by_column, sent = sent[: nx - 1], sent[nx - 1 :]
    send(last, sent)

    g_came = [swap_dp(v, 1) for v in g_parts[1:]]
    fence(g_parts[1:])

    sent = call(
        functools.partial(second_back_kernel, nx, size),
        "second_back",
        [shape(2 * size, rows)] * (nx - 1),
        [near, *by_column],
    )
    columns = [swap(v, xo) for xo, v in enumerate(sent, 1)]

    sum_shapes = [shape(feats, n * toks), shape(2, 16, toks, dtype=F32)]

    def combine(parts, refs, carried, outs, final):
        return call(
            functools.partial(combine_kernel, n, cap, feats, parts, bool(carried), final),
            "combine",
            outs,
            [me_arr, ids_t, metas, *refs, *carried],
            scalars=1,
        )

    parts = [(0, 0, 0), (nx, 1, 0)] + [(k, i, 0) for i, k in enumerate(far, 2)]
    sums = combine(
        parts,
        [own, near, *[straight[k] for k in far]],
        [],
        sum_shapes,
        False,
    )

    others = ny - 1
    out_spec = pl.BlockSpec((1, block, tile_w), lambda i: (0, 0, i))
    pairs = lambda ours, theirs: [v for both in zip(ours, theirs) for v in both]
    grad_gate_w, grad_up_w, _ = run(
        functools.partial(rest_weights_kernel, rows, others),
        "weights_rest",
        [shape(1, block, h)] * 2 + [shape(8, 128, dtype=F32)],
        [my_core, *pairs(x_parts[1:], x_came), *pairs(g_parts[1:], g_came), w_part],
        [smem()] + [x_spec] * (2 * others) + [column_w] * (2 * others) + [part_spec],
        [out_spec, out_spec, whole((8, 128))],
        grid=(h // tile_w,),
        scratch=[
            pltpu.VMEM((block, 2 * others * rows), BF16),
            pltpu.VMEM((2 * others * rows, tile_w), BF16),
        ],
    )

    parts = []
    for i in range(nx - 1):
        parts += [(i + 1, i, 0), (nx + i + 1, i, size)]
    sums = combine(parts, columns, sums, sum_shapes, False)
    summed, gg = combine(
        [(k, i, 0) for i, k in enumerate(last)],
        [straight[k] for k in last],
        sums,
        [shape(feats, n * toks), shape(2, toks)],
        True,
    )
    return summed.T, grad_gate_w, grad_up_w, gg.T


def solution(mesh):
    placed = (
        P(("dp", "expert"), None),
        P(("dp", "expert"), None),
        P(("dp", "expert"), None),
        P(("dp", "expert"), None),
        P("expert", None, None),
        P("expert", None, None),
        P("expert", None, None),
    )
    return jax.shard_map(
        local,
        mesh=mesh,
        in_specs=placed,
        out_specs=(
            P("dp", "expert"),
            P("expert", "dp", None),
            P("expert", "dp", None),
            P(("dp", "expert"), None),
        ),
        check_vma=False,
    )
```
